512 devices in a mesh: section: 2 (over x_hi), ep: 128 (over y, z, core), tp: 2 (over x_lo).
Axes of the slice: x: 4 (x_hi: 2, x_lo: 2; x = x_hi * 2 + x_lo), y: 8, z: 8, core: 2. Of those that a mesh axis runs over, the one named last changes fastest.
Arguments:
- section_rows: bfloat16 [2, 512, 7168], P('section', 'ep', 'tp'), may hold values from -6 to 6
- routes: int32 [2, 512, 4], P('section', 'ep'), may hold values from 0 to 7, all different within a row; in each aligned block of 4 rows (0 to 3, 4 to 7, ..., all dimensions but the last counted through in order) at most 3 rows name the same one
- route_weights: float32 [2, 512, 4], P('section', 'ep'), may hold values from 0.1 to 0.5
- in_gain: bfloat16 [2, 7168], P('section', 'tp'), may hold values from 0.099609375 to 1.8984375
- gate_up: bfloat16 [2, 128, 7168, 256], P('section', 'ep', 'tp'), may hold values from -0.0625 to 0.0625
- down: bfloat16 [2, 128, 128, 7168], P('section', 'ep', None, 'tp'), may hold values from -0.125 to 0.125
- out_gain: bfloat16 [2, 7168], P('section', 'tp'), may hold values from 0.099609375 to 1.8984375
Outputs:
- layer_out: bfloat16 [2, 512, 7168], P('section', 'ep', 'tp')
- handed: bfloat16 [2, 512, 7168], P('section', 'ep', 'tp')
The draws below stay inside these ranges and needn't reach their ends.
Inputs may be any that keep to these rules, and one draw needn't show every extreme that they name: `routes`: each row names 4 different experts. Among the 4 rows of one index of ep (aligned blocks of rows, both groups counted in order), no expert is named by more than 3 rows, a bound that some block reaches.
All inputs are finite; a program needn't handle non-finite values.
Results may differ from the reference program's by a relative error of at most 0.012.
Values may be sent and summed in bfloat16 or wider, within the bound.
No kernel may reach another device: no remote copies, remote signals or barrier semaphores. Data moves between devices by JAX's collectives and lax.ppermute only.
A program may use at most 64 MiB of HBM per device.

```python
import math
import jax
import jax.numpy as jnp
import numpy as np
from jax import lax

D = 7168
HB = 2048
EXP_SPAN = 16
ROWS_DEV = 4
HPART = 128
EXPERTS = 8
TOPK = 4
ROWS = 512
MOST = 3
N_EP = 128


def levels(key, dims, shards, least, top_value):
    loudness, own = 1.0, jax.random.fold_in(key, 6)
    for axis_at, blocks in shards:
        steps = jnp.exp(jax.random.uniform(jax.random.fold_in(own, axis_at), (blocks,), jnp.float32, least / len(shards), top_value / len(shards)))
        loudness = loudness * jnp.repeat(steps, dims[axis_at] // blocks).reshape([-1 if axis == axis_at else 1 for axis in range(len(dims))])
    return loudness


def assign_block(rng, own, number, rows, count, top, limit, slope):
    order = jax.random.permutation(rng, count)
    heavy_load, ordinary = load_shares(count, rows * top, limit, slope, True), load_shares(count, rows * top, limit, slope, False)
    places = jnp.arange(count)

    def named(tallies, offset_by):
        used = int((tallies > 0).sum())
        fixed = max(1, used // 4)
        moved = fixed + (places - fixed + offset_by * (used - fixed)) % max(1, count - fixed)
        return jnp.zeros((count,), jnp.int32).at[order[jnp.where(places < fixed, places, moved)]].set(jnp.asarray(tallies, jnp.int32))

    tallies = jnp.where(number % 4 == 0, named(heavy_load, number // 4), named(ordinary, number - number // 4 - 1))
    mixed = jax.random.permutation(jax.random.fold_in(own, 3), count)
    donor, sink = mixed[0:count // 2 * 2:2], mixed[1:count // 2 * 2:2]
    margin = jnp.minimum(tallies[donor] - 1, limit - tallies[sink]) // 2
    margin = jnp.where((donor == order[0]) | (sink == order[0]) | (tallies[sink] == 0), 0, jnp.maximum(margin, 0))
    moved = jax.random.randint(jax.random.fold_in(own, 4), (count // 2,), 0, 1 << 20) % (margin + 1)
    tallies = tallies.at[donor].add(-moved).at[sink].add(moved)
    items = jnp.searchsorted(jnp.cumsum(tallies), jnp.arange(rows * top), side="right").astype(jnp.int32)
    table = items.reshape(top, rows).T
    table = table[jax.random.permutation(jax.random.fold_in(own, 1), rows)]
    offset_by = jax.random.randint(jax.random.fold_in(own, 2), (rows, 1), 0, top)
    return jnp.take_along_axis(table, (jnp.arange(top)[None, :] + offset_by) % top, axis=1)


def load_shares(count, total, most, skew, full):
    portions = [(1 << 20) // math.isqrt(grade ** skew) + 1 for grade in range(1, count + 1)]
    largest = most if full else min(most, max(-(-total // count), total * portions[0] // sum(portions)))
    least = 1 if total - largest >= count - 1 else 0
    given, spare = [largest] + [least] * (count - 1), total - largest - least * (count - 1)
    while spare > 0:
        movable = [i for i in range(1, count) if given[i] < largest] or [i for i in range(1, count) if given[i] < most]
        pool, budget = sum([portions[i] for i in movable]), spare
        for i in movable:
            extra = min(most - given[i], max(1, budget * portions[i] // pool), spare)
            given[i] = given[i] + extra
            spare = spare - extra
    return np.array(given)


def scatter_about(stream_key, extent, spread, bound, pieces=(), kind=jnp.bfloat16):
    level = levels(stream_key, extent, pieces, -0.22, 0.18) if pieces else 1.0
    values = jax.random.normal(stream_key, extent, jnp.float32) * spread * level
    return jnp.minimum(jnp.maximum(values, -bound), bound).astype(kind)


def setup_inputs(seed: int = 0) -> dict:
    key_list = jax.random.split(jax.random.key(seed), 8)
    section_rows = scatter_about(key_list[0], (2, ROWS, D), 1.0, 6.0, ((0, 2), (1, 128), (2, 2)))
    routes_keys = jax.random.split(jax.random.fold_in(key_list[1], 1), 2 * ROWS // ROWS_DEV)
    routes_turns = jax.random.permutation(jax.random.fold_in(key_list[1], 3), 2 * ROWS // ROWS_DEV)
    routes = jax.vmap(lambda own, number: assign_block(jax.random.fold_in(key_list[1], 2), own, number, ROWS_DEV, EXPERTS, TOPK, MOST, 2))(routes_keys, routes_turns).reshape((2, ROWS, TOPK))
    route_weights = jnp.clip(0.1 + 0.4 * jax.random.uniform(key_list[2], (2, ROWS, TOPK), jnp.float32) ** levels(key_list[2], (2, ROWS, TOPK), ((0, 2), (1, 128)), -0.2, 0.2), 0.1, 0.5)
    in_gain = jnp.clip(1.0 + 0.18 * jax.random.normal(key_list[3], (2, D), jnp.float32), 0.099609375, 1.8984375).astype(jnp.bfloat16)
    gate_up = scatter_about(key_list[4], (2, EXPERTS * EXP_SPAN, D, 2 * HPART), D ** -0.5, 0.0625, ((0, 2), (1, 128), (2, 2)))
    down = scatter_about(key_list[5], (2, EXPERTS * EXP_SPAN, HPART, D), HB ** -0.5, 0.125, ((0, 2), (1, 128), (3, 2)))
    out_gain = jnp.clip(1.0 + 0.18 * jax.random.normal(key_list[6], (2, D), jnp.float32), 0.099609375, 1.8984375).astype(jnp.bfloat16)
    return dict(section_rows=section_rows, routes=routes, route_weights=route_weights, in_gain=in_gain, gate_up=gate_up, down=down, out_gain=out_gain)


def rms_scale(values):
    return lax.rsqrt(lax.optimization_barrier(jnp.mean(values * values, axis=1)) + 1e-06)

def moe_layer(inputs, route_ids, weights, gain, gate_proj, down_proj):
    values = inputs.astype(jnp.float32)
    normed = (values * rms_scale(values)[:, None] * gain.astype(jnp.float32)[None, :]).astype(jnp.bfloat16)
    blocks = route_ids.reshape(N_EP, ROWS_DEV * TOPK)
    expert_ids = jnp.arange(EXPERTS, dtype=jnp.int32)

    def ranks(block):
        onehot = (block[:, None] == expert_ids[None, :]).astype(jnp.int32)
        return lax.optimization_barrier(jnp.sum((jnp.cumsum(onehot, axis=0) - 1) * onehot, axis=1)).astype(jnp.int32)
    slot_rank = lax.map(ranks, blocks)
    source = jnp.arange(N_EP, dtype=jnp.int32)[:, None]
    row_index = source * ROWS_DEV + jnp.arange(ROWS_DEV * TOPK, dtype=jnp.int32)[None, :] // TOPK
    slot_ids = ((blocks * N_EP + source) * MOST + slot_rank).reshape(-1)
    span = N_EP * MOST
    row_of = jnp.full((EXPERTS * span,), ROWS, jnp.int32).at[slot_ids].set(row_index.reshape(-1))
    weight_of = jnp.zeros((EXPERTS * span,), jnp.float32).at[slot_ids].set(weights.reshape(-1).astype(jnp.float32))
    padded = jnp.concatenate([normed, jnp.zeros((1, D), jnp.bfloat16)], axis=0)
    gate_all = gate_proj.reshape(EXPERTS, EXP_SPAN, D, 2 * HPART)
    down_all = down_proj.reshape(EXPERTS, EXP_SPAN, HPART, D)

    def expert_step(total, expert):
        index = lax.dynamic_slice_in_dim(row_of, expert * span, span)
        scales = lax.dynamic_slice_in_dim(weight_of, expert * span, span)
        gathered = padded[index]
        gate_here = gate_all[expert]
        down_here = down_all[expert]
        summed = jnp.zeros((span, D), jnp.float32)
        for block in range(EXP_SPAN):
            both = jnp.dot(gathered, gate_here[block], preferred_element_type=jnp.float32)
            hidden = (jax.nn.silu(both[:, :HPART]) * both[:, HPART:]).astype(jnp.bfloat16)
            part = jnp.dot(hidden, down_here[block], preferred_element_type=jnp.float32).astype(jnp.bfloat16)
            summed = summed + part.astype(jnp.float32)
        total = total.at[index].add(summed * scales[:, None])
        return (total, None)
    start = jnp.zeros((ROWS + 1, D), jnp.float32)
    total, unused = lax.scan(expert_step, start, jnp.arange(EXPERTS, dtype=jnp.int32))
    return (values + total[:ROWS]).astype(jnp.bfloat16)

def reference(section_rows, routes, route_weights, in_gain, gate_up, down, out_gain):
    outputs = []
    closings = []
    for group in range(2):
        layer = moe_layer(section_rows[group], routes[group], route_weights[group], in_gain[group], gate_up[group], down[group])
        residual = layer.astype(jnp.float32)
        closing = (residual * rms_scale(residual)[:, None] * out_gain[group].astype(jnp.float32)[None, :]).astype(jnp.bfloat16)
        outputs.append(layer)
        closings.append(closing)
    layer_out = jnp.stack(outputs, axis=0)
    handed = jnp.stack([closings[1], closings[0]], axis=0)
    return (layer_out, handed)
```

```python
import jax
import jax.numpy as jnp
from jax import lax
from jax.sharding import PartitionSpec as P

EXTRA = 128


def crossed_groups(ep, span, first):
    along_y = [[y * span + i for y in range(ep // span)] for i in range(span)]
    along_z = [
        [y * span + z * 2 + c for z in range(span // 2)] for y in range(ep // span) for c in range(2)
    ]
    return [g for g in along_z if g[0] % 2 == first] + [g for g in along_y if g[0] % 2 != first]


def traded(block, groups):
    return lax.all_to_all(block, "ep", 0, 0, axis_index_groups=groups, tiled=True)


def spread(block, groups):
    count = len(groups[0])
    copies = jnp.broadcast_to(block[None], (count,) + block.shape)
    got = traded(copies, groups)
    return got.reshape((-1,) + block.shape[1:])


def collected(block, groups):
    count = len(groups[0])
    parts = block.reshape((count, block.shape[0] // count) + block.shape[1:])
    got = traded(parts, groups)
    return jnp.sum(got.astype(jnp.float32), axis=0)


def body(section_rows, routes, route_weights, in_gain, gate_up, down, out_gain):
    bf16, f32 = jnp.bfloat16, jnp.float32
    rows = section_rows[0]
    row_count, half_width = rows.shape
    ep = lax.axis_size("ep")
    width = half_width * lax.axis_size("tp")
    hidden_units = down.shape[2]
    span = 16
    expert_count = ep // span
    near, far = crossed_groups(ep, span, 0), crossed_groups(ep, span, 1)
    expert = lax.axis_index("ep") // span
    other_core = [(i, i ^ 1) for i in range(ep)]
    swap = [(0, 1), (1, 0)]

    gate_own, down_own = gate_up[0, 0], down[0, 0]
    gate_other = lax.ppermute(gate_own, "ep", other_core)
    down_other = lax.ppermute(down_own, "ep", other_core)
    gain_other = lax.ppermute(out_gain, "section", swap)[0].astype(f32)

    named = routes[0][:, :, None] == jnp.arange(expert_count, dtype=jnp.int32)[None, None, :]
    dense = jnp.sum(jnp.where(named, route_weights[0][:, :, None], 0.0), axis=1)
    high = lax.reduce_precision(dense, 8, 7)
    low = dense - high
    extra = jnp.concatenate(
        [high, low, jnp.zeros((row_count, EXTRA - 2 * expert_count), f32)], axis=1
    ).astype(bf16)
    payload = jnp.concatenate([rows, extra], axis=1)

    gathered = spread(spread(payload, near), far)
    values = gathered[:, :half_width].astype(f32)
    tail = gathered[:, half_width:].astype(f32)
    lane = jnp.arange(EXTRA, dtype=jnp.int32)[None, :]
    mine = (lane == expert) | (lane == expert + expert_count)
    weight = jnp.sum(jnp.where(mine, tail, 0.0), axis=1)
    squares = jnp.sum(values * values, axis=1)
    squares = squares + lax.ppermute(squares, "tp", swap)
    scale = lax.rsqrt(squares / width + 1e-06)
    scaled = (values * in_gain[0].astype(f32)[None, :]).astype(bf16)
    partial = jnp.concatenate(
        [
            jnp.dot(scaled, gate_own, preferred_element_type=f32),
            jnp.dot(scaled, gate_other, preferred_element_type=f32),
        ],
        axis=1,
    )
    totals = partial + lax.ppermute(partial.astype(bf16), "tp", swap).astype(f32)
    totals = totals * scale[:, None]
    hu = hidden_units
    hidden = [
        (jax.nn.silu(totals[:, at : at + hu]) * totals[:, at + hu : at + 2 * hu] * weight[:, None]).astype(bf16)
        for at in (0, 2 * hu)
    ]
    parts = (
        jnp.dot(hidden[0], down_own, preferred_element_type=f32)
        + jnp.dot(hidden[1], down_other, preferred_element_type=f32)
    ).astype(bf16)
    mixture = collected(collected(parts, far).astype(bf16), near)
    layer_out = (rows.astype(f32) + mixture).astype(bf16)
    mine_out = layer_out.astype(f32)
    my_squares = jnp.sum(mine_out * mine_out, axis=1)
    far_squares = lax.ppermute(my_squares, ("section", "tp"), [(0, 3), (3, 0), (1, 2), (2, 1)])
    theirs = lax.ppermute(layer_out, "section", swap).astype(f32)
    total = jnp.sum(theirs * theirs, axis=1) + far_squares
    handed = (theirs * lax.rsqrt(total / width + 1e-06)[:, None] * gain_other[None, :]).astype(bf16)
    return (layer_out[None], handed[None])


def solution(mesh):
    return jax.shard_map(
        body,
        mesh=mesh,
        in_specs=(
            P("section", "ep", "tp"),
            P("section", "ep", None),
            P("section", "ep", None),
            P("section", "tp"),
            P("section", "ep", "tp", None),
            P("section", "ep", None, "tp"),
            P("section", "tp"),
        ),
        out_specs=(P("section", "ep", "tp"), P("section", "ep", "tp")),
        check_vma=False,
    )
```

```python
import functools

import jax
import jax.numpy as jnp
from jax import lax
from jax.experimental import pallas as pl
from jax.experimental.pallas import tpu as pltpu
from jax.sharding import PartitionSpec as P

BF16, F32 = jnp.bfloat16, jnp.float32
SPAN = 16
ALONG = 8
ROWS = 4
MOST = 3
EXPERTS = 8
EXTRA = 128
WIDE = ALONG * ROWS
TIGHT = ALONG * MOST
PARAMS = dict(compiler_params=pltpu.CompilerParams(vmem_limit_bytes=24 * 1024 * 1024))


def crossed_groups(ep, first):
    along_y = [[y * SPAN + i for y in range(ep // SPAN)] for i in range(SPAN)]
    along_z = [
        [y * SPAN + z * 2 + c for z in range(SPAN // 2)] for y in range(ep // SPAN) for c in range(2)
    ]
    return [g for g in along_z if g[0] % 2 == first] + [g for g in along_y if g[0] % 2 != first]


def traded(block, groups):
    return lax.all_to_all(block, "ep", 0, 0, axis_index_groups=groups, tiled=True)


def index(shape, axis):
    return lax.broadcasted_iota(jnp.int32, shape, axis).astype(F32)


def split(at, count):
    whole = jnp.floor((at + 0.5) * (1.0 / count))
    return whole, at - whole * count


def announce(info_ref, rows_ref, routes_ref, weights_ref, out_ref, back_ref):
    crossing = info_ref[0] == 0
    half_width = rows_ref.shape[1]
    lane = lax.broadcasted_iota(jnp.int32, (ROWS, EXTRA), 1)
    routes, weights = routes_ref[...], weights_ref[...]
    dense = jnp.zeros((ROWS, EXTRA), F32)
    later = jnp.zeros((ROWS, EXTRA), F32)
    for k in range(routes.shape[1]):
        dense += jnp.where(lane == routes[:, k : k + 1], weights[:, k : k + 1], 0.0)
        later += jnp.where(lane == routes[:, k : k + 1] + EXPERTS, weights[:, k : k + 1], 0.0)
    high = dense.astype(BF16).astype(F32)
    low = later - later.astype(BF16).astype(F32)
    extra = jnp.where(lane < EXPERTS, high, low)
    named = jnp.where(dense > 0.0, 1.0, 0.0)
    codes, before = [], jnp.zeros((1, EXTRA), F32)
    for r in range(ROWS):
        codes.append(jnp.where(named[r : r + 1] > 0.5, before, -1.0))
        before = before + named[r : r + 1]
    rows = rows_ref[...].astype(F32)
    target, slot = split(index((WIDE, 1), 0), ROWS)
    pick = jnp.where(index((WIDE, EXTRA), 1) == target, 1.0, 0.0)
    body = jnp.zeros((WIDE, half_width), F32)
    tail = jnp.zeros((WIDE, EXTRA), F32)
    for r in range(ROWS):
        code = jnp.sum(pick * codes[r], axis=1, keepdims=True)
        here = jnp.where(jnp.where(crossing, r * 1.0, code) == slot, 1.0, 0.0)
        body += here * rows[r : r + 1]
        tail += here * extra[r : r + 1]
    out_ref[:, :half_width] = body.astype(BF16)
    out_ref[:, half_width:] = tail.astype(BF16)
    table = jnp.concatenate(codes + [jnp.full((8 - ROWS, EXTRA), -1.0, F32)], axis=0)
    target, slot = split(index((EXTRA, WIDE), 1), ROWS)
    spread = jnp.where(index((EXTRA, WIDE), 0) == target, 1.0, 0.0).astype(BF16)
    found = jnp.dot(table.astype(BF16), spread, preferred_element_type=F32)
    found = jnp.where(crossing, index((8, WIDE), 0), found)
    back_ref[...] = jnp.where(found == slot[:8], 1.0, 0.0).astype(BF16)


def sort_rows(info_ref, rows_ref, out_ref, back_ref):
    crossing = info_ref[0] == 0
    half_width = rows_ref.shape[1] - EXTRA
    total = ALONG * TIGHT
    tail = rows_ref[:, half_width:].astype(F32)
    named = jnp.where((tail > 0.0) & (index((WIDE, EXTRA), 1) < EXPERTS - 0.5), 1.0, 0.0)
    one, two = index((WIDE, WIDE), 0), index((WIDE, WIDE), 1)
    ahead = jnp.where((split(one, ROWS)[0] == split(two, ROWS)[0]) & (two < one), 1.0, 0.0)
    rank = jnp.dot(ahead.astype(BF16), named.astype(BF16), preferred_element_type=F32)
    code = jnp.where(named > 0.5, rank, -1.0).astype(BF16)

    def matrix(found, at, to):
        source, slot = split(split(at, TIGHT)[1], MOST)
        block, row = split(to, ROWS)
        found = jnp.where(crossing, found, row)
        return jnp.where((block == source) & (found == slot), 1.0, 0.0).astype(BF16)

    target = split(index((total, EXTRA), 0), TIGHT)[0]
    pick = jnp.where(index((total, EXTRA), 1) == target, 1.0, 0.0).astype(BF16)
    found = lax.dot_general(pick, code, (((1,), (1,)), ((), ())), preferred_element_type=F32)
    forth = matrix(found, index((total, WIDE), 0), index((total, WIDE), 1))
    target = split(index((EXTRA, total), 1), TIGHT)[0]
    pick = jnp.where(index((EXTRA, total), 0) == target, 1.0, 0.0).astype(BF16)
    found = jnp.dot(code, pick, preferred_element_type=F32)
    back_ref[...] = matrix(found, index((WIDE, total), 1), index((WIDE, total), 0))
    rows = rows_ref[...]
    for t in range(ALONG):
        out_ref[t] = jnp.dot(
            forth[t * TIGHT : (t + 1) * TIGHT], rows, preferred_element_type=F32
        ).astype(BF16)


def gate(rows_ref, gain_ref, own_ref, other_ref, kept_ref, sent_ref, squares):
    step = pl.program_id(0)
    cols = own_ref.shape[1]

    @pl.when(step == 0)
    def _():
        kept_ref[...] = jnp.zeros_like(kept_ref)
        squares[...] = jnp.zeros_like(squares)

    values = rows_ref[...].astype(F32)
    squares[...] += jnp.sum(values * values, axis=1, keepdims=True)
    scaled = (values * gain_ref[...].astype(F32)).astype(BF16)
    kept_ref[:, :cols] += jnp.dot(scaled, own_ref[...], preferred_element_type=F32)
    kept_ref[:, cols : 2 * cols] += jnp.dot(scaled, other_ref[...], preferred_element_type=F32)

    @pl.when(step == pl.num_programs(0) - 1)
    def _():
        total = squares[...]
        high = total.astype(BF16).astype(F32)
        lane = lax.broadcasted_iota(jnp.int32, total.shape, 1)
        pieces = jnp.where(lane == 0, high, jnp.where(lane == 1, total - high, 0.0))
        kept_ref[:, 2 * cols :] = total
        sent_ref[:, : 2 * cols] = kept_ref[:, : 2 * cols].astype(BF16)
        sent_ref[:, 2 * cols :] = pieces.astype(BF16)


def expert(width, info_ref, tail_ref, kept_ref, got_ref, own_ref, other_ref, out_ref, hidden):
    units = own_ref.shape[0]

    @pl.when(pl.program_id(0) == 0)
    def _():
        which = info_ref[1]
        tail = tail_ref[...].astype(F32)
        lane = lax.broadcasted_iota(jnp.int32, tail.shape, 1)
        mine = (lane == which) | (lane == which + EXPERTS)
        weight = jnp.sum(jnp.where(mine, tail, 0.0), axis=1, keepdims=True)
        far = jnp.sum(got_ref[:, 4 * units :].astype(F32), axis=1, keepdims=True)
        squares = kept_ref[:, 4 * units : 4 * units + 1] + far
        scale = lax.rsqrt(squares * (1.0 / width) + 1e-06)
        for at in range(2):
            lo = 2 * units * at
            a = (kept_ref[:, lo : lo + units] + got_ref[:, lo : lo + units].astype(F32)) * scale
            lo += units
            b = (kept_ref[:, lo : lo + units] + got_ref[:, lo : lo + units].astype(F32)) * scale
            value = a / (1.0 + jnp.exp(-a)) * b * weight
            hidden[:, at * units : (at + 1) * units] = value.astype(BF16)

    out_ref[...] = (
        jnp.dot(hidden[:, :units], own_ref[...], preferred_element_type=F32)
        + jnp.dot(hidden[:, units:], other_ref[...], preferred_element_type=F32)
    ).astype(BF16)


def gather_parts(back_ref, parts_ref, out_ref):
    out_ref[...] = jnp.dot(back_ref[...], parts_ref[...], preferred_element_type=F32).astype(BF16)


def finish(back_ref, parts_ref, rows_ref, out_ref, squares_ref):
    mixture = jnp.dot(back_ref[...], parts_ref[...], preferred_element_type=F32)[:ROWS]
    layer = (rows_ref[...].astype(F32) + mixture).astype(BF16)
    out_ref[...] = layer
    values = layer.astype(F32)
    squares_ref[...] = jnp.broadcast_to(
        jnp.sum(values * values, axis=1, keepdims=True), squares_ref.shape
    )


def close(width, theirs_ref, far_ref, gain_ref, out_ref):
    values = theirs_ref[...].astype(F32)
    total = jnp.sum(values * values, axis=1, keepdims=True) + far_ref[:, :1]
    scale = lax.rsqrt(total * (1.0 / width) + 1e-06)
    out_ref[...] = (values * scale * gain_ref[...].astype(F32)).astype(BF16)


def local(kernel, outs, *args, smem=0):
    specs = [
        pl.BlockSpec(memory_space=pltpu.SMEM if at < smem else pltpu.VMEM) for at in range(len(args))
    ]
    out_specs = [pl.BlockSpec(memory_space=pltpu.VMEM) for _ in outs]
    return pl.pallas_call(kernel, out_shape=outs, in_specs=specs, out_specs=out_specs, **PARAMS)(*args)


def shape(*dims, dtype=BF16):
    return jax.ShapeDtypeStruct(dims, dtype)


def body(section_rows, routes, route_weights, in_gain, gate_up, down, out_gain):
    rows = section_rows[0]
    half_width = rows.shape[1]
    ep = lax.axis_size("ep")
    width = half_width * lax.axis_size("tp")
    units = down.shape[2]
    cols = gate_up.shape[3]
    near, far = crossed_groups(ep, 0), crossed_groups(ep, 1)
    place = lax.axis_index("ep")
    info = jnp.stack([place % 2, place // SPAN]).astype(jnp.int32)
    other_core = [(i, i ^ 1) for i in range(ep)]
    swap = [(0, 1), (1, 0)]
    full = half_width + EXTRA
    total = ALONG * TIGHT

    gate_own, down_own = gate_up[0, 0], down[0, 0]
    gate_other = lax.ppermute(gate_own, "ep", other_core)
    down_other = lax.ppermute(down_own, "ep", other_core)
    gain_other = lax.ppermute(out_gain, "section", swap)

    leaving, home_back = local(
        announce, [shape(WIDE, full), shape(8, WIDE)], info, rows, routes[0], route_weights[0], smem=1
    )
    met = traded(leaving.reshape(ALONG, ROWS, full), near).reshape(WIDE, full)
    sorted_rows, far_back = local(
        sort_rows, [shape(ALONG, TIGHT, full), shape(WIDE, total)], info, met, smem=1
    )
    gathered = traded(sorted_rows, far).reshape(total, full)
    gathered, gain_other = lax.optimization_barrier((gathered, gain_other))

    steps = 4
    deep = half_width // steps
    kept, sent = pl.pallas_call(
        gate,
        grid=(steps,),
        out_shape=[shape(total, 2 * cols + EXTRA, dtype=F32), shape(total, 2 * cols + EXTRA)],
        in_specs=[
            pl.BlockSpec((total, deep), lambda k: (0, k)),
            pl.BlockSpec((1, deep), lambda k: (0, k)),
            pl.BlockSpec((deep, cols), lambda k: (k, 0)),
            pl.BlockSpec((deep, cols), lambda k: (k, 0)),
        ],
        out_specs=[pl.BlockSpec((total, 2 * cols + EXTRA), lambda k: (0, 0))] * 2,
        scratch_shapes=[pltpu.VMEM((total, EXTRA), F32)],
        **PARAMS,
    )(gathered, in_gain, gate_own, gate_other)
    got = lax.ppermute(sent, "tp", swap)
    parts = pl.pallas_call(
        functools.partial(expert, width),
        grid=(steps,),
        out_shape=shape(total, half_width),
        in_specs=[
            pl.BlockSpec(memory_space=pltpu.SMEM),
            pl.BlockSpec((total, EXTRA), lambda k: (0, half_width // EXTRA)),
            pl.BlockSpec((total, 2 * cols + EXTRA), lambda k: (0, 0)),
            pl.BlockSpec((total, 2 * cols + EXTRA), lambda k: (0, 0)),
            pl.BlockSpec((units, deep), lambda k: (0, k)),
            pl.BlockSpec((units, deep), lambda k: (0, k)),
        ],
        out_specs=pl.BlockSpec((total, deep), lambda k: (0, k)),
        scratch_shapes=[pltpu.VMEM((total, 2 * units), BF16)],
        **PARAMS,
    )(info, gathered, kept, got, down_own, down_other)
    returned = traded(parts.reshape(ALONG, TIGHT, half_width), far).reshape(total, half_width)
    (summed,) = local(gather_parts, [shape(WIDE, half_width)], far_back, returned)
    home = traded(summed.reshape(ALONG, ROWS, half_width), near).reshape(WIDE, half_width)
    layer_out, squares = local(
        finish, [shape(ROWS, half_width), shape(ROWS, EXTRA, dtype=F32)], home_back, home, rows
    )
    theirs = lax.ppermute(layer_out, "section", swap)
    far_squares = lax.ppermute(squares, ("section", "tp"), [(0, 3), (3, 0), (1, 2), (2, 1)])
    (handed,) = local(
        functools.partial(close, width), [shape(ROWS, half_width)], theirs, far_squares, gain_other
    )
    return (layer_out[None], handed[None])


def solution(mesh):
    return jax.shard_map(
        body,
        mesh=mesh,
        in_specs=(
            P("section", "ep", "tp"),
            P("section", "ep", None),
            P("section", "ep", None),
            P("section", "tp"),
            P("section", "ep", "tp", None),
            P("section", "ep", None, "tp"),
            P("section", "tp"),
        ),
        out_specs=(P("section", "ep", "tp"), P("section", "ep", "tp")),
        check_vma=False,
    )
```

```python
import functools

import jax
import jax.numpy as jnp
import numpy as np
from jax import lax
from jax.experimental import pallas as pl
from jax.experimental.pallas import tpu as pltpu
from jax.sharding import PartitionSpec as P

BF16, F32 = jnp.bfloat16, jnp.float32
SPAN = 16
ALONG = 8
ROWS = 4
MOST = 3
EXPERTS = 8
EXTRA = 128
WIDE = ALONG * ROWS
TIGHT = ALONG * MOST
MIB = 1024 * 1024


def crossed_groups(ep, first):
    along_y = [[y * SPAN + i for y in range(ep // SPAN)] for i in range(SPAN)]
    along_z = [
        [y * SPAN + z * 2 + c for z in range(SPAN // 2)] for y in range(ep // SPAN) for c in range(2)
    ]
    return [g for g in along_z if g[0] % 2 == first] + [g for g in along_y if g[0] % 2 != first]


def traded(block, groups):
    return lax.all_to_all(block, "ep", 0, 0, axis_index_groups=groups, tiled=True)


def index(shape, axis):
    return lax.broadcasted_iota(jnp.int32, shape, axis).astype(F32)


def split(at, count):
    whole = jnp.floor((at + 0.5) * (1.0 / count))
    return whole, at - whole * count


def announce(info_ref, rows_ref, dense_ref, out_ref, back_ref):
    crossing = info_ref[0] == 0
    half_width = rows_ref.shape[1]
    lane = index((ROWS, EXTRA), 1)
    dense = dense_ref[...]
    high = dense.astype(BF16).astype(F32)
    extra = jnp.where(lane < EXPERTS, high, dense - high)
    named = jnp.where((dense > 0.0) & (lane < EXPERTS), 1.0, 0.0)
    codes, before = [], jnp.zeros((1, EXTRA), F32)
    for r in range(ROWS):
        codes.append(jnp.where(named[r : r + 1] > 0.5, before, -1.0))
        before = before + named[r : r + 1]
    rows = rows_ref[...].astype(F32)
    target, slot = split(index((WIDE, 1), 0), ROWS)
    pick = jnp.where(index((WIDE, EXTRA), 1) == target, 1.0, 0.0)
    body = jnp.zeros((WIDE, half_width), F32)
    tail = jnp.zeros((WIDE, EXTRA), F32)
    for r in range(ROWS):
        code = jnp.sum(pick * codes[r], axis=1, keepdims=True)
        here = jnp.where(jnp.where(crossing, r * 1.0, code) == slot, 1.0, 0.0)
        body += here * rows[r : r + 1]
        tail += here * extra[r : r + 1]
    out_ref[:, :half_width] = body.astype(BF16)
    out_ref[:, half_width:] = tail.astype(BF16)
    table = jnp.concatenate(codes + [jnp.full((8 - ROWS, EXTRA), -1.0, F32)], axis=0)
    target, slot = split(index((EXTRA, WIDE), 1), ROWS)
    spread = jnp.where(index((EXTRA, WIDE), 0) == target, 1.0, 0.0).astype(BF16)
    found = jnp.dot(table.astype(BF16), spread, preferred_element_type=F32)
    found = jnp.where(crossing, index((8, WIDE), 0), found)
    back_ref[...] = jnp.where(found == slot[:8], 1.0, 0.0).astype(BF16)


def sort_rows(info_ref, rows_ref, out_ref, back_ref, staged, sems):
    crossing = info_ref[0] == 0
    half_width = rows_ref.shape[1] - EXTRA
    total = ALONG * TIGHT
    tail = rows_ref[:, half_width:].astype(F32)
    named = jnp.where((tail > 0.0) & (index((WIDE, EXTRA), 1) < EXPERTS - 0.5), 1.0, 0.0)
    one, two = index((WIDE, WIDE), 0), index((WIDE, WIDE), 1)
    ahead = jnp.where((split(one, ROWS)[0] == split(two, ROWS)[0]) & (two < one), 1.0, 0.0)
    rank = jnp.dot(ahead.astype(BF16), named.astype(BF16), preferred_element_type=F32)
    code = jnp.where(named > 0.5, rank, -1.0).astype(BF16)

    def matrix(found, at, to):
        source, slot = split(split(at, TIGHT)[1], MOST)
        block, row = split(to, ROWS)
        found = jnp.where(crossing, found, row)
        return jnp.where((block == source) & (found == slot), 1.0, 0.0).astype(BF16)

    target = split(index((total, EXTRA), 0), TIGHT)[0]
    pick = jnp.where(index((total, EXTRA), 1) == target, 1.0, 0.0).astype(BF16)
    found = lax.dot_general(pick, code, (((1,), (1,)), ((), ())), preferred_element_type=F32)
    forth = matrix(found, index((total, WIDE), 0), index((total, WIDE), 1))
    target = split(index((EXTRA, total), 1), TIGHT)[0]
    pick = jnp.where(index((EXTRA, total), 0) == target, 1.0, 0.0).astype(BF16)
    found = jnp.dot(code, pick, preferred_element_type=F32)
    back_ref[...] = matrix(found, index((WIDE, total), 1), index((WIDE, total), 0))
    rows = rows_ref[...]
    copies = []
    for t in range(ALONG):
        staged[t] = jnp.dot(
            forth[t * TIGHT : (t + 1) * TIGHT], rows, preferred_element_type=F32
        ).astype(BF16)
        copies.append(pltpu.make_async_copy(staged.at[t], out_ref.at[t], sems.at[t]))
        copies[t].start()
    for copy in copies:
        copy.wait()


def gate(rows_ref, gain_ref, own_ref, other_ref, kept_ref, sent_ref, scaled, squares):
    half_width, cols = own_ref.shape
    deep = half_width // 4
    for k in range(4):
        at = slice(k * deep, (k + 1) * deep)
        values = rows_ref[:, at].astype(F32)
        part = jnp.sum(values * values, axis=1, keepdims=True)
        squares[...] = jnp.broadcast_to(part, squares.shape) + (squares[...] if k else 0.0)
        scaled[:, at] = (values * gain_ref[:, at].astype(F32)).astype(BF16)
    for at, weights in ((0, own_ref), (cols, other_ref)):
        sums = jnp.dot(scaled[...], weights[...], preferred_element_type=F32)
        kept_ref[:, at : at + cols] = sums
        sent_ref[:, at : at + cols] = sums.astype(BF16)
    total = squares[...]
    high = total.astype(BF16).astype(F32)
    lane = lax.broadcasted_iota(jnp.int32, total.shape, 1)
    pieces = jnp.where(lane == 0, high, jnp.where(lane == 1, total - high, 0.0))
    kept_ref[:, 2 * cols :] = total
    sent_ref[:, 2 * cols :] = pieces.astype(BF16)


def expert(width, info_ref, rows_ref, kept_ref, got_ref, down_ref, out_ref):
    units, half_width = down_ref.shape[0] // 2, down_ref.shape[1]
    which = info_ref[1]
    tail = rows_ref[:, half_width:].astype(F32)
    lane = lax.broadcasted_iota(jnp.int32, tail.shape, 1)
    mine = (lane == which) | (lane == which + EXPERTS)
    weight = jnp.sum(jnp.where(mine, tail, 0.0), axis=1, keepdims=True)
    far = jnp.sum(got_ref[:, 4 * units :].astype(F32), axis=1, keepdims=True)
    squares = kept_ref[:, 4 * units : 4 * units + 1] + far
    scale = lax.rsqrt(squares * (1.0 / width) + 1e-06)
    hidden = []
    for at in range(2):
        lo = 2 * units * at
        a = (kept_ref[:, lo : lo + units] + got_ref[:, lo : lo + units].astype(F32)) * scale
        lo += units
        b = (kept_ref[:, lo : lo + units] + got_ref[:, lo : lo + units].astype(F32)) * scale
        hidden.append((a / (1.0 + jnp.exp(-a)) * b * weight).astype(BF16))
    both = jnp.concatenate(hidden, axis=1)
    deep = half_width // 4
    for k in range(4):
        at = slice(k * deep, (k + 1) * deep)
        out_ref[:, at] = jnp.dot(both, down_ref[:, at], preferred_element_type=F32).astype(BF16)


def gather_parts(back_ref, parts_ref, out_ref):
    out_ref[...] = jnp.dot(back_ref[...], parts_ref[...], preferred_element_type=F32).astype(BF16)


def finish(back_ref, parts_ref, rows_ref, out_ref, squares_ref):
    mixture = jnp.dot(back_ref[...], parts_ref[...], preferred_element_type=F32)[:ROWS]
    layer = (rows_ref[...].astype(F32) + mixture).astype(BF16)
    out_ref[...] = layer
    values = layer.astype(F32)
    squares_ref[...] = jnp.broadcast_to(
        jnp.sum(values * values, axis=1, keepdims=True), squares_ref.shape
    )


def close(width, theirs_ref, far_ref, gain_ref, out_ref):
    values = theirs_ref[...].astype(F32)
    total = jnp.sum(values * values, axis=1, keepdims=True) + far_ref[:, :1]
    scale = lax.rsqrt(total * (1.0 / width) + 1e-06)
    out_ref[...] = (values * scale * gain_ref[...].astype(F32)).astype(BF16)


def local(kernel, outs, *args, spaces=None, out_spaces=None, scratch=(), vmem=24 * MIB):
    spaces = spaces or [pltpu.VMEM] * len(args)
    out_spaces = out_spaces or [pltpu.VMEM] * len(outs)
    return pl.pallas_call(
        kernel,
        out_shape=outs,
        in_specs=[pl.BlockSpec(memory_space=space) for space in spaces],
        out_specs=[pl.BlockSpec(memory_space=space) for space in out_spaces],
        scratch_shapes=list(scratch),
        compiler_params=pltpu.CompilerParams(vmem_limit_bytes=vmem),
    )(*args)


def shape(*dims, dtype=BF16):
    return jax.ShapeDtypeStruct(dims, dtype)


def body(section_rows, routes, route_weights, in_gain, gate_up, down, out_gain):
    rows = section_rows[0]
    half_width = rows.shape[1]
    ep = lax.axis_size("ep")
    width = half_width * lax.axis_size("tp")
    units = down.shape[2]
    cols = gate_up.shape[3]
    near, far = crossed_groups(ep, 0), crossed_groups(ep, 1)
    place = lax.axis_index("ep")
    info = jnp.stack([place % 2, place // SPAN]).astype(jnp.int32)
    other_core = [(i, i ^ 1) for i in range(ep)]
    swap = [(0, 1), (1, 0)]
    full = half_width + EXTRA
    total = ALONG * TIGHT

    gate_own, down_own = gate_up[0, 0], down[0, 0]
    gate_other = lax.ppermute(gate_own, "ep", other_core)
    down_other = lax.ppermute(down_own, "ep", other_core)
    gain_other = lax.ppermute(out_gain, "section", swap)

    down_all = jnp.concatenate([down_own, down_other], axis=0)

    slots = np.arange(EXTRA)
    slots = np.where(slots < 2 * EXPERTS, slots % EXPERTS, -1).astype(np.int32)
    named = routes[0][:, :, None] == slots[None, None, :]
    leaving, home_back = local(
        announce,
        [shape(WIDE, full), shape(8, WIDE)],
        info,
        rows,
        jnp.sum(jnp.where(named, route_weights[0][:, :, None], 0.0), axis=1),
        spaces=[pltpu.SMEM] + [pltpu.VMEM] * 2,
    )
    met = traded(leaving.reshape(ALONG, ROWS, full), near).reshape(WIDE, full)
    sorted_rows, far_back = local(
        sort_rows,
        [shape(ALONG, TIGHT, full), shape(WIDE, total)],
        info,
        met,
        spaces=[pltpu.SMEM, pltpu.VMEM],
        out_spaces=[pltpu.HBM, pltpu.VMEM],
        scratch=[pltpu.VMEM((ALONG, TIGHT, full), BF16), pltpu.SemaphoreType.DMA((ALONG,))],
        vmem=53 * MIB,
    )
    gathered = traded(sorted_rows, far).reshape(total, full)
    gathered, gain_other = lax.optimization_barrier((gathered, gain_other))
    kept, sent = local(
        gate,
        [shape(total, 2 * cols + EXTRA, dtype=F32), shape(total, 2 * cols + EXTRA)],
        gathered,
        in_gain,
        gate_own,
        gate_other,
        scratch=[pltpu.VMEM((total, half_width), BF16), pltpu.VMEM((total, EXTRA), F32)],
    )
    got = lax.ppermute(sent, "tp", swap)
    (parts,) = local(
        functools.partial(expert, width),
        [shape(total, half_width)],
        info,
        gathered,
        kept,
        got,
        down_all,
        spaces=[pltpu.SMEM] + [pltpu.VMEM] * 4,
    )
    returned = traded(parts.reshape(ALONG, TIGHT, half_width), far).reshape(total, half_width)
    (summed,) = local(gather_parts, [shape(WIDE, half_width)], far_back, returned)
    home = traded(summed.reshape(ALONG, ROWS, half_width), near).reshape(WIDE, half_width)
    layer_out, squares = local(
        finish, [shape(ROWS, half_width), shape(ROWS, EXTRA, dtype=F32)], home_back, home, rows
    )
    theirs = lax.ppermute(layer_out, "section", swap)
    far_squares = lax.ppermute(squares, ("section", "tp"), [(0, 3), (3, 0), (1, 2), (2, 1)])
    (handed,) = local(
        functools.partial(close, width), [shape(ROWS, half_width)], theirs, far_squares, gain_other
    )
    return (layer_out[None], handed[None])


def solution(mesh):
    return jax.shard_map(
        body,
        mesh=mesh,
        in_specs=(
            P("section", "ep", "tp"),
            P("section", "ep", None),
            P("section", "ep", None),
            P("section", "tp"),
            P("section", "ep", "tp", None),
            P("section", "ep", None, "tp"),
            P("section", "tp"),
        ),
        out_specs=(P("section", "ep", "tp"), P("section", "ep", "tp")),
        check_vma=False,
    )
```

```python
import functools

import jax
import jax.numpy as jnp
from jax import lax
from jax.experimental import pallas as pl
from jax.experimental.pallas import tpu as pltpu
from jax.sharding import PartitionSpec as P

BF16, F32 = jnp.bfloat16, jnp.float32
SPAN = 16
ALONG = 8
ROWS = 4
MOST = 3
EXPERTS = 8
EXTRA = 128
WIDE = ALONG * ROWS
TIGHT = ALONG * MOST
MIB = 1024 * 1024
CHUNK = 1024


def crossed_groups(ep, first):
    along_y = [[y * SPAN + i for y in range(ep // SPAN)] for i in range(SPAN)]
    along_z = [
        [y * SPAN + z * 2 + c for z in range(SPAN // 2)] for y in range(ep // SPAN) for c in range(2)
    ]
    return [g for g in along_z if g[0] % 2 == first] + [g for g in along_y if g[0] % 2 != first]


def traded(block, groups):
    return lax.all_to_all(block, "ep", 0, 0, axis_index_groups=groups, tiled=True)


def index(shape, axis):
    return lax.broadcasted_iota(jnp.int32, shape, axis).astype(F32)


def split(at, count):
    whole = jnp.floor((at + 0.5) * (1.0 / count))
    return whole, at - whole * count


def announce(rows_ref, routes_ref, weights_ref, out_ref):
    half_width = rows_ref.shape[1]
    row = lax.broadcasted_iota(jnp.int32, (ROWS, EXTRA), 0)
    lane = lax.broadcasted_iota(jnp.int32, (ROWS, EXTRA), 1)
    dense = jnp.zeros((ROWS, EXTRA), F32)
    for r in range(ROWS):
        for k in range(routes_ref.shape[1]):
            name = routes_ref[r, k]
            here = (row == r) & ((lane == name) | (lane == name + EXPERTS))
            dense += jnp.where(here, weights_ref[r, k], 0.0)
    high = dense.astype(BF16).astype(F32)
    extra = jnp.where(lane < EXPERTS, high, dense - high).astype(BF16)
    rows = rows_ref[...]
    for t in range(ALONG):
        out_ref[t, :, :half_width] = rows
        out_ref[t, :, half_width:] = extra


def sort_rows(info_ref, rows_ref, out_ref, back_ref, staged, sems):
    crossing, which = info_ref[0] == 0, info_ref[1].astype(F32)
    half_width = rows_ref.shape[1] - EXTRA
    total = ALONG * TIGHT
    tail = rows_ref[:, half_width:].astype(F32)
    named = jnp.where((tail > 0.0) & (index((WIDE, EXTRA), 1) < EXPERTS - 0.5), 1.0, 0.0)
    one, two = index((WIDE, WIDE), 0), index((WIDE, WIDE), 1)
    ahead = jnp.where((split(one, ROWS)[0] == split(two, ROWS)[0]) & (two < one), 1.0, 0.0)
    rank = jnp.dot(ahead.astype(BF16), named.astype(BF16), preferred_element_type=F32)
    code = jnp.where(named > 0.5, rank, -1.0).astype(BF16)

    def matrix(found, at, to):
        source, slot = split(split(at, TIGHT)[1], MOST)
        block = split(to, ROWS)[0]
        return jnp.where((block == source) & (found == slot), 1.0, 0.0).astype(BF16)

    def pick(at, to):
        target = jnp.where(crossing, split(at, TIGHT)[0], which)
        return jnp.where(to == target, 1.0, 0.0).astype(BF16)

    chosen = pick(index((total, 1), 0), index((total, EXTRA), 1))
    found = lax.dot_general(chosen, code, (((1,), (1,)), ((), ())), preferred_element_type=F32)
    forth = matrix(found, index((total, 1), 0), index((1, WIDE), 1))
    copies = []
    for k, lo in enumerate(range(0, half_width + EXTRA, CHUNK)):
        at = pl.ds(lo, min(CHUNK, half_width + EXTRA - lo))
        staged[:, at] = jnp.dot(forth, rows_ref[:, at], preferred_element_type=F32).astype(BF16)
        copies.append(pltpu.make_async_copy(staged.at[:, at], out_ref.at[:, at], sems.at[k]))
        copies[k].start()
    chosen = pick(index((1, total), 1), index((EXTRA, total), 0))
    found = jnp.dot(code, chosen, preferred_element_type=F32)
    back_ref[...] = matrix(found, index((1, total), 1), index((WIDE, 1), 0))
    for copy in copies:
        copy.wait()


def gate(
    rows_ref, gain_ref, own_ref, other_hbm, kept_ref, sent_ref, scaled, squares, other_ref, sem
):
    half_width, cols = own_ref.shape
    copy = pltpu.make_async_copy(other_hbm, other_ref, sem)
    copy.start()
    deep = half_width // 4
    for k in range(4):
        at = slice(k * deep, (k + 1) * deep)
        values = rows_ref[:, at].astype(F32)
        part = jnp.sum(values * values, axis=1, keepdims=True)
        squares[...] = jnp.broadcast_to(part, squares.shape) + (squares[...] if k else 0.0)
        scaled[:, at] = (values * gain_ref[:, at].astype(F32)).astype(BF16)
    for at, weights in ((0, own_ref), (cols, other_ref)):
        if at:
            copy.wait()
        sums = jnp.dot(scaled[...], weights[...], preferred_element_type=F32)
        kept_ref[:, at : at + cols] = sums
        sent_ref[:, at : at + cols] = sums.astype(BF16)
    total = squares[...]
    high = total.astype(BF16).astype(F32)
    lane = lax.broadcasted_iota(jnp.int32, total.shape, 1)
    pieces = jnp.where(lane == 0, high, jnp.where(lane == 1, total - high, 0.0))
    kept_ref[:, 2 * cols :] = total
    sent_ref[:, 2 * cols :] = pieces.astype(BF16)


def expert(width, info_ref, rows_ref, kept_ref, got_ref, down_ref, out_ref):
    units, half_width = down_ref.shape[0] // 2, down_ref.shape[1]
    which = info_ref[1]
    tail = rows_ref[:, half_width:].astype(F32)
    lane = lax.broadcasted_iota(jnp.int32, tail.shape, 1)
    mine = (lane == which) | (lane == which + EXPERTS)
    weight = jnp.sum(jnp.where(mine, tail, 0.0), axis=1, keepdims=True)
    far = jnp.sum(got_ref[:, 4 * units :].astype(F32), axis=1, keepdims=True)
    squares = kept_ref[:, 4 * units : 4 * units + 1] + far
    scale = lax.rsqrt(squares * (1.0 / width) + 1e-06)
    hidden = []
    for at in range(2):
        lo = 2 * units * at
        a = (kept_ref[:, lo : lo + units] + got_ref[:, lo : lo + units].astype(F32)) * scale
        lo += units
        b = (kept_ref[:, lo : lo + units] + got_ref[:, lo : lo + units].astype(F32)) * scale
        hidden.append((a / (1.0 + jnp.exp(-a)) * b * weight).astype(BF16))
    both = jnp.concatenate(hidden, axis=1)
    deep = half_width // 4
    for k in range(4):
        at = slice(k * deep, (k + 1) * deep)
        out_ref[:, at] = jnp.dot(both, down_ref[:, at], preferred_element_type=F32).astype(BF16)


def gather_parts(back_ref, parts_ref, out_ref):
    out_ref[...] = jnp.dot(back_ref[...], parts_ref[...], preferred_element_type=F32).astype(BF16)


def finish(parts_ref, rows_ref, out_ref, squares_ref):
    mixture = parts_ref[0].astype(F32)
    for t in range(1, ALONG):
        mixture += parts_ref[t].astype(F32)
    layer = (rows_ref[...].astype(F32) + mixture).astype(BF16)
    out_ref[...] = layer
    values = layer.astype(F32)
    squares_ref[...] = jnp.broadcast_to(
        jnp.sum(values * values, axis=1, keepdims=True), squares_ref.shape
    )


def close(width, theirs_ref, far_ref, gain_ref, out_ref):
    values = theirs_ref[...].astype(F32)
    total = jnp.sum(values * values, axis=1, keepdims=True) + far_ref[:, :1]
    scale = lax.rsqrt(total * (1.0 / width) + 1e-06)
    out_ref[...] = (values * scale * gain_ref[...].astype(F32)).astype(BF16)


def local(kernel, outs, *args, spaces=None, out_spaces=None, scratch=(), vmem=24 * MIB):
    spaces = spaces or [pltpu.VMEM] * len(args)
    out_spaces = out_spaces or [pltpu.VMEM] * len(outs)
    return pl.pallas_call(
        kernel,
        out_shape=outs,
        in_specs=[pl.BlockSpec(memory_space=space) for space in spaces],
        out_specs=[pl.BlockSpec(memory_space=space) for space in out_spaces],
        scratch_shapes=list(scratch),
        compiler_params=pltpu.CompilerParams(vmem_limit_bytes=vmem),
    )(*args)


def shape(*dims, dtype=BF16):
    return jax.ShapeDtypeStruct(dims, dtype)


def body(section_rows, routes, route_weights, in_gain, gate_up, down, out_gain):
    rows = section_rows[0]
    half_width = rows.shape[1]
    ep = lax.axis_size("ep")
    width = half_width * lax.axis_size("tp")
    units = down.shape[2]
    cols = gate_up.shape[3]
    near, far = crossed_groups(ep, 0), crossed_groups(ep, 1)
    place = lax.axis_index("ep")
    info = jnp.stack([place % 2, place // SPAN]).astype(jnp.int32)
    other_core = [(i, i ^ 1) for i in range(ep)]
    swap = [(0, 1), (1, 0)]
    full = half_width + EXTRA
    total = ALONG * TIGHT

    gate_own, down_own = gate_up[0, 0], down[0, 0]
    gate_other = lax.ppermute(gate_own, "ep", other_core)
    down_other = lax.ppermute(down_own, "ep", other_core)
    gain_other = lax.ppermute(out_gain, "section", swap)

    down_all = jnp.concatenate([down_own, down_other], axis=0)

    (leaving,) = local(
        announce,
        [shape(ALONG, ROWS, full)],
        rows,
        routes[0],
        route_weights[0],
        spaces=[pltpu.VMEM, pltpu.SMEM, pltpu.SMEM],
        vmem=60 * MIB,
    )
    met = traded(leaving, near).reshape(WIDE, full)
    sorted_rows, far_back = local(
        sort_rows,
        [shape(total, full), shape(WIDE, total)],
        info,
        met,
        spaces=[pltpu.SMEM, pltpu.VMEM],
        out_spaces=[pltpu.HBM, pltpu.VMEM],
        scratch=[pltpu.VMEM((total, full), BF16), pltpu.SemaphoreType.DMA((-(-full // CHUNK),))],
        vmem=53 * MIB,
    )
    gathered = traded(sorted_rows.reshape(ALONG, TIGHT, full), far).reshape(total, full)
    gathered, gain_other = lax.optimization_barrier((gathered, gain_other))
    kept, sent = local(
        gate,
        [shape(total, 2 * cols + EXTRA, dtype=F32), shape(total, 2 * cols + EXTRA)],
        gathered,
        in_gain,
        gate_own,
        gate_other,
        spaces=[pltpu.VMEM] * 3 + [pl.ANY],
        scratch=[
            pltpu.VMEM((total, half_width), BF16),
            pltpu.VMEM((total, EXTRA), F32),
            pltpu.VMEM((half_width, cols), BF16),
            pltpu.SemaphoreType.DMA,
        ],
    )
    got = lax.ppermute(sent, "tp", swap)
    (parts,) = local(
        functools.partial(expert, width),
        [shape(total, half_width)],
        info,
        gathered,
        kept,
        got,
        down_all,
        spaces=[pltpu.SMEM] + [pltpu.VMEM] * 4,
    )
    returned = traded(parts.reshape(ALONG, TIGHT, half_width), far).reshape(total, half_width)
    (summed,) = local(gather_parts, [shape(WIDE, half_width)], far_back, returned)
    home = traded(summed.reshape(ALONG, ROWS, half_width), near)
    layer_out, squares = local(
        finish, [shape(ROWS, half_width), shape(ROWS, EXTRA, dtype=F32)], home, rows
    )
    theirs = lax.ppermute(layer_out, "section", swap)
    far_squares = lax.ppermute(squares, ("section", "tp"), [(0, 3), (3, 0), (1, 2), (2, 1)])
    (handed,) = local(
        functools.partial(close, width), [shape(ROWS, half_width)], theirs, far_squares, gain_other
    )
    return (layer_out[None], handed[None])


def solution(mesh):
    return jax.shard_map(
        body,
        mesh=mesh,
        in_specs=(
            P("section", "ep", "tp"),
            P("section", "ep", None),
            P("section", "ep", None),
            P("section", "tp"),
            P("section", "ep", "tp", None),
            P("section", "ep", None, "tp"),
            P("section", "tp"),
        ),
        out_specs=(P("section", "ep", "tp"), P("section", "ep", "tp")),
        check_vma=False,
    )
```

```python
import functools

import jax
import jax.numpy as jnp
from jax import lax
from jax.experimental import pallas as pl
from jax.experimental.pallas import tpu as pltpu
from jax.sharding import PartitionSpec as P

BF16, F32 = jnp.bfloat16, jnp.float32
SPAN = 16
ALONG = 8
ROWS = 4
MOST = 3
EXPERTS = 8
EXTRA = 128
WIDE = ALONG * ROWS
TIGHT = ALONG * MOST
MIB = 1024 * 1024
CHUNK = 1024


def crossed_groups(ep, first):
    along_y = [[y * SPAN + i for y in range(ep // SPAN)] for i in range(SPAN)]
    along_z = [
        [y * SPAN + z * 2 + c for z in range(SPAN // 2)] for y in range(ep // SPAN) for c in range(2)
    ]
    return [g for g in along_z if g[0] % 2 == first] + [g for g in along_y if g[0] % 2 != first]


def traded(block, groups):
    return lax.all_to_all(block, "ep", 0, 0, axis_index_groups=groups, tiled=True)


def index(shape, axis):
    return lax.broadcasted_iota(jnp.int32, shape, axis).astype(F32)


def split(at, count):
    whole = jnp.floor((at + 0.5) * (1.0 / count))
    return whole, at - whole * count


def announce(rows_ref, routes_ref, weights_ref, out_ref):
    half_width = rows_ref.shape[1]
    row = lax.broadcasted_iota(jnp.int32, (ROWS, EXTRA), 0)
    lane = lax.broadcasted_iota(jnp.int32, (ROWS, EXTRA), 1)
    dense = jnp.zeros((ROWS, EXTRA), F32)
    for r in range(ROWS):
        for k in range(routes_ref.shape[1]):
            name = routes_ref[r, k]
            here = (row == r) & ((lane == name) | (lane == name + EXPERTS))
            dense += jnp.where(here, weights_ref[r, k], 0.0)
    high = dense.astype(BF16).astype(F32)
    extra = jnp.where(lane < EXPERTS, high, dense - high).astype(BF16)
    rows = rows_ref[...]
    for t in range(ALONG):
        out_ref[t, :, :half_width] = rows
        out_ref[t, :, half_width:] = extra


def sort_rows(info_ref, rows_ref, out_ref, back_ref, staged, sems):
    crossing, which = info_ref[0] == 0, info_ref[1].astype(F32)
    half_width = rows_ref.shape[1] - EXTRA
    total = ALONG * TIGHT
    tail = rows_ref[:, half_width:].astype(F32)
    named = jnp.where((tail > 0.0) & (index((WIDE, EXTRA), 1) < EXPERTS - 0.5), 1.0, 0.0)
    one, two = index((WIDE, WIDE), 0), index((WIDE, WIDE), 1)
    ahead = jnp.where((split(one, ROWS)[0] == split(two, ROWS)[0]) & (two < one), 1.0, 0.0)
    rank = jnp.dot(ahead.astype(BF16), named.astype(BF16), preferred_element_type=F32)
    code = jnp.where(named > 0.5, rank, -1.0).astype(BF16)

    def matrix(found, at, to):
        source, slot = split(split(at, TIGHT)[1], MOST)
        block = split(to, ROWS)[0]
        return jnp.where((block == source) & (found == slot), 1.0, 0.0).astype(BF16)

    def pick(at, to):
        target = jnp.where(crossing, split(at, TIGHT)[0], which)
        return jnp.where(to == target, 1.0, 0.0).astype(BF16)

    chosen = pick(index((total, 1), 0), index((total, EXTRA), 1))
    found = lax.dot_general(chosen, code, (((1,), (1,)), ((), ())), preferred_element_type=F32)
    forth = matrix(found, index((total, 1), 0), index((1, WIDE), 1))
    copies = []
    for k, lo in enumerate(range(0, half_width + EXTRA, CHUNK)):
        at = pl.ds(lo, min(CHUNK, half_width + EXTRA - lo))
        staged[:, at] = jnp.dot(forth, rows_ref[:, at], preferred_element_type=F32).astype(BF16)
        copies.append(pltpu.make_async_copy(staged.at[:, at], out_ref.at[:, at], sems.at[k]))
        copies[k].start()
    chosen = pick(index((1, total), 1), index((EXTRA, total), 0))
    found = jnp.dot(code, chosen, preferred_element_type=F32)
    back_ref[...] = matrix(found, index((1, total), 1), index((WIDE, 1), 0))
    for copy in copies:
        copy.wait()


def gate(rows_ref, gain_ref, own_ref, other_ref, kept_ref, sent_ref, squares):
    half_width, cols = own_ref.shape
    deep = half_width // 7
    for k in range(7):
        at = slice(k * deep, (k + 1) * deep)
        values = rows_ref[:, at].astype(F32)
        part = jnp.sum(values * values, axis=1, keepdims=True)
        squares[...] = jnp.broadcast_to(part, squares.shape) + (squares[...] if k else 0.0)
        scaled = (values * gain_ref[:, at].astype(F32)).astype(BF16)
        for lo, weights in ((0, own_ref), (cols, other_ref)):
            sums = jnp.dot(scaled, weights[at, :], preferred_element_type=F32)
            kept_ref[:, lo : lo + cols] = sums + (kept_ref[:, lo : lo + cols] if k else 0.0)
    sent_ref[:, : 2 * cols] = kept_ref[:, : 2 * cols].astype(BF16)
    total = squares[...]
    high = total.astype(BF16).astype(F32)
    lane = lax.broadcasted_iota(jnp.int32, total.shape, 1)
    pieces = jnp.where(lane == 0, high, jnp.where(lane == 1, total - high, 0.0))
    kept_ref[:, 2 * cols :] = total
    sent_ref[:, 2 * cols :] = pieces.astype(BF16)


def expert(width, info_ref, rows_ref, kept_ref, got_ref, down_ref, out_ref):
    units, half_width = down_ref.shape[0] // 2, down_ref.shape[1]
    which = info_ref[1]
    tail = rows_ref[:, half_width:].astype(F32)
    lane = lax.broadcasted_iota(jnp.int32, tail.shape, 1)
    mine = (lane == which) | (lane == which + EXPERTS)
    weight = jnp.sum(jnp.where(mine, tail, 0.0), axis=1, keepdims=True)
    far = jnp.sum(got_ref[:, 4 * units :].astype(F32), axis=1, keepdims=True)
    squares = kept_ref[:, 4 * units : 4 * units + 1] + far
    scale = lax.rsqrt(squares * (1.0 / width) + 1e-06)
    hidden = []
    for at in range(2):
        lo = 2 * units * at
        a = (kept_ref[:, lo : lo + units] + got_ref[:, lo : lo + units].astype(F32)) * scale
        lo += units
        b = (kept_ref[:, lo : lo + units] + got_ref[:, lo : lo + units].astype(F32)) * scale
        hidden.append((a / (1.0 + jnp.exp(-a)) * b * weight).astype(BF16))
    both = jnp.concatenate(hidden, axis=1)
    deep = half_width // 4
    for k in range(4):
        at = slice(k * deep, (k + 1) * deep)
        out_ref[:, at] = jnp.dot(both, down_ref[:, at], preferred_element_type=F32).astype(BF16)


def gather_parts(back_ref, parts_ref, out_ref):
    out_ref[...] = jnp.dot(back_ref[...], parts_ref[...], preferred_element_type=F32).astype(BF16)


def finish(parts_ref, rows_ref, out_ref, sent_ref):
    half_width = rows_ref.shape[1]
    mixture = parts_ref[0].astype(F32)
    for t in range(1, ALONG):
        mixture += parts_ref[t].astype(F32)
    layer = (rows_ref[...].astype(F32) + mixture).astype(BF16)
    out_ref[...] = layer
    values = layer.astype(F32)
    total = jnp.sum(values * values, axis=1, keepdims=True)
    high = total.astype(BF16).astype(F32)
    lane = lax.broadcasted_iota(jnp.int32, (ROWS, EXTRA), 1)
    pieces = jnp.where(lane == 0, high, jnp.where(lane == 1, total - high, 0.0)).astype(BF16)
    for to in range(sent_ref.shape[0]):
        sent_ref[to, :, :half_width] = layer
        sent_ref[to, :, half_width:] = pieces


def close(width, info_ref, got_ref, gain_ref, out_ref):
    half_width = gain_ref.shape[1]
    values = got_ref[info_ref[2], :, :half_width].astype(F32)
    far = got_ref[info_ref[3], :, half_width:].astype(F32)
    total = jnp.sum(values * values, axis=1, keepdims=True) + jnp.sum(far, axis=1, keepdims=True)
    scale = lax.rsqrt(total * (1.0 / width) + 1e-06)
    out_ref[...] = (values * scale * gain_ref[...].astype(F32)).astype(BF16)


def local(kernel, outs, *args, spaces=None, out_spaces=None, scratch=(), vmem=24 * MIB):
    spaces = spaces or [pltpu.VMEM] * len(args)
    out_spaces = out_spaces or [pltpu.VMEM] * len(outs)
    return pl.pallas_call(
        kernel,
        out_shape=outs,
        in_specs=[pl.BlockSpec(memory_space=space) for space in spaces],
        out_specs=[pl.BlockSpec(memory_space=space) for space in out_spaces],
        scratch_shapes=list(scratch),
        compiler_params=pltpu.CompilerParams(vmem_limit_bytes=vmem),
    )(*args)


def shape(*dims, dtype=BF16):
    return jax.ShapeDtypeStruct(dims, dtype)


def body(section_rows, routes, route_weights, in_gain, gate_up, down, out_gain):
    rows = section_rows[0]
    half_width = rows.shape[1]
    ep = lax.axis_size("ep")
    width = half_width * lax.axis_size("tp")
    units = down.shape[2]
    cols = gate_up.shape[3]
    near, far = crossed_groups(ep, 0), crossed_groups(ep, 1)
    place = lax.axis_index("ep")
    crossed, side = 1 - lax.axis_index("section"), lax.axis_index("tp")
    info = jnp.stack(
        [place % 2, place // SPAN, crossed * 2 + side, crossed * 2 + 1 - side]
    ).astype(jnp.int32)
    other_core = [(i, i ^ 1) for i in range(ep)]
    swap = [(0, 1), (1, 0)]
    full = half_width + EXTRA
    total = ALONG * TIGHT

    gate_own, down_own = gate_up[0, 0], down[0, 0]
    gate_other = lax.ppermute(gate_own, "ep", other_core)
    down_other = lax.ppermute(down_own, "ep", other_core)
    gain_other = lax.ppermute(out_gain, "section", swap)

    down_all = jnp.concatenate([down_own, down_other], axis=0)

    (leaving,) = local(
        announce,
        [shape(ALONG, ROWS, full)],
        rows,
        routes[0],
        route_weights[0],
        spaces=[pltpu.VMEM, pltpu.SMEM, pltpu.SMEM],
        vmem=60 * MIB,
    )
    met = traded(leaving, near).reshape(WIDE, full)
    sorted_rows, far_back = local(
        sort_rows,
        [shape(total, full), shape(WIDE, total)],
        info,
        met,
        spaces=[pltpu.SMEM, pltpu.VMEM],
        out_spaces=[pltpu.HBM, pltpu.VMEM],
        scratch=[pltpu.VMEM((total, full), BF16), pltpu.SemaphoreType.DMA((-(-full // CHUNK),))],
        vmem=53 * MIB,
    )
    gathered = traded(sorted_rows.reshape(ALONG, TIGHT, full), far).reshape(total, full)
    gathered, gain_other = lax.optimization_barrier((gathered, gain_other))
    kept, sent = local(
        gate,
        [shape(total, 2 * cols + EXTRA, dtype=F32), shape(total, 2 * cols + EXTRA)],
        gathered,
        in_gain,
        gate_own,
        gate_other,
        scratch=[pltpu.VMEM((total, EXTRA), F32)],
    )
    got = lax.ppermute(sent, "tp", swap)
    (parts,) = local(
        functools.partial(expert, width),
        [shape(total, half_width)],
        info,
        gathered,
        kept,
        got,
        down_all,
        spaces=[pltpu.SMEM] + [pltpu.VMEM] * 4,
    )
    returned = traded(parts.reshape(ALONG, TIGHT, half_width), far).reshape(total, half_width)
    (summed,) = local(gather_parts, [shape(WIDE, half_width)], far_back, returned)
    home = traded(summed.reshape(ALONG, ROWS, half_width), near)
    layer_out, leaving = local(
        finish, [shape(ROWS, half_width), shape(4, ROWS, full)], home, rows
    )
    got = lax.all_to_all(leaving, ("section", "tp"), 0, 0, tiled=True)
    (handed,) = local(
        functools.partial(close, width),
        [shape(ROWS, half_width)],
        info,
        got,
        gain_other,
        spaces=[pltpu.SMEM] + [pltpu.VMEM] * 2,
    )
    return (layer_out[None], handed[None])


def solution(mesh):
    return jax.shard_map(
        body,
        mesh=mesh,
        in_specs=(
            P("section", "ep", "tp"),
            P("section", "ep", None),
            P("section", "ep", None),
            P("section", "tp"),
            P("section", "ep", "tp", None),
            P("section", "ep", None, "tp"),
            P("section", "tp"),
        ),
        out_specs=(P("section", "ep", "tp"), P("section", "ep", "tp")),
        check_vma=False,
    )
```

```python
import functools

import jax
import jax.numpy as jnp
from jax import lax
from jax.experimental import pallas as pl
from jax.experimental.pallas import tpu as pltpu
from jax.sharding import PartitionSpec as P

BF16, F32 = jnp.bfloat16, jnp.float32
SPAN = 16
ALONG = 8
ROWS = 4
MOST = 3
EXPERTS = 8
EXTRA = 128
WIDE = ALONG * ROWS
TIGHT = ALONG * MOST
MIB = 1024 * 1024
CHUNK = 1024


def crossed_groups(ep, first):
    along_y = [[y * SPAN + i for y in range(ep // SPAN)] for i in range(SPAN)]
    along_z = [
        [y * SPAN + z * 2 + c for z in range(SPAN // 2)] for y in range(ep // SPAN) for c in range(2)
    ]
    return [g for g in along_z if g[0] % 2 == first] + [g for g in along_y if g[0] % 2 != first]


def traded(block, groups):
    return lax.all_to_all(block, "ep", 0, 0, axis_index_groups=groups, tiled=True)


def index(shape, axis):
    return lax.broadcasted_iota(jnp.int32, shape, axis).astype(F32)


def split(at, count):
    whole = jnp.floor((at + 0.5) * (1.0 / count))
    return whole, at - whole * count


def announce(rows_hbm, routes_ref, weights_ref, out_hbm, extra_ref, sems):
    half_width = rows_hbm.shape[1]
    copies = []
    for t in range(ALONG):
        target = out_hbm.at[t, :, pl.ds(0, half_width)]
        copies.append(pltpu.make_async_copy(rows_hbm, target, sems.at[t]))
        copies[t].start()
    row = lax.broadcasted_iota(jnp.int32, (ROWS, EXTRA), 0)
    lane = lax.broadcasted_iota(jnp.int32, (ROWS, EXTRA), 1)
    dense = jnp.zeros((ROWS, EXTRA), F32)
    for r in range(ROWS):
        for k in range(routes_ref.shape[1]):
            name = routes_ref[r, k]
            here = (row == r) & ((lane == name) | (lane == name + EXPERTS))
            dense += jnp.where(here, weights_ref[r, k], 0.0)
    high = dense.astype(BF16).astype(F32)
    extra_ref[...] = jnp.where(lane < EXPERTS, high, dense - high).astype(BF16)
    for t in range(ALONG):
        target = out_hbm.at[t, :, pl.ds(half_width, EXTRA)]
        copies.append(pltpu.make_async_copy(extra_ref, target, sems.at[ALONG + t]))
        copies[ALONG + t].start()
    for copy in copies:
        copy.wait()


def sort_rows(info_ref, rows_ref, out_ref, back_ref, staged, sems):
    crossing, which = info_ref[0] == 0, info_ref[1].astype(F32)
    half_width = rows_ref.shape[1] - EXTRA
    total = ALONG * TIGHT
    tail = rows_ref[:, half_width:].astype(F32)
    named = jnp.where((tail > 0.0) & (index((WIDE, EXTRA), 1) < EXPERTS - 0.5), 1.0, 0.0)
    one, two = index((WIDE, WIDE), 0), index((WIDE, WIDE), 1)
    ahead = jnp.where((split(one, ROWS)[0] == split(two, ROWS)[0]) & (two < one), 1.0, 0.0)
    rank = jnp.dot(ahead.astype(BF16), named.astype(BF16), preferred_element_type=F32)
    code = jnp.where(named > 0.5, rank, -1.0).astype(BF16)

    def matrix(found, at, to):
        source, slot = split(split(at, TIGHT)[1], MOST)
        block = split(to, ROWS)[0]
        return jnp.where((block == source) & (found == slot), 1.0, 0.0).astype(BF16)

    def pick(at, to):
        target = jnp.where(crossing, split(at, TIGHT)[0], which)
        return jnp.where(to == target, 1.0, 0.0).astype(BF16)

    chosen = pick(index((total, 1), 0), index((total, EXTRA), 1))
    found = lax.dot_general(chosen, code, (((1,), (1,)), ((), ())), preferred_element_type=F32)
    forth = matrix(found, index((total, 1), 0), index((1, WIDE), 1))
    copies = []
    for k, lo in enumerate(range(0, half_width + EXTRA, CHUNK)):
        at = pl.ds(lo, min(CHUNK, half_width + EXTRA - lo))
        staged[:, at] = jnp.dot(forth, rows_ref[:, at], preferred_element_type=F32).astype(BF16)
        copies.append(pltpu.make_async_copy(staged.at[:, at], out_ref.at[:, at], sems.at[k]))
        copies[k].start()
    chosen = pick(index((1, total), 1), index((EXTRA, total), 0))
    found = jnp.dot(code, chosen, preferred_element_type=F32)
    back_ref[...] = matrix(found, index((1, total), 1), index((WIDE, 1), 0))
    for copy in copies:
        copy.wait()


def gate(
    rows_ref, gain_ref, own_ref, other_hbm, kept_ref, sent_ref, squares_ref, scaled_ref, other_ref, sem
):
    copy = pltpu.make_async_copy(other_hbm, other_ref, sem)
    copy.start()
    half_width, cols = own_ref.shape[0], kept_ref.shape[1]
    rows = rows_ref.shape[0]
    deep = half_width // 7
    for k in range(7):
        at = slice(k * deep, (k + 1) * deep)
        values = rows_ref[:, at].astype(F32)
        part = jnp.sum(values * values, axis=1, keepdims=True)
        squares_ref[...] = jnp.broadcast_to(part, squares_ref.shape) + (
            squares_ref[...] if k else 0.0
        )
        scaled = (values * gain_ref[:, at].astype(F32)).astype(BF16)
        scaled_ref[:, at] = scaled
        sums = jnp.dot(scaled, own_ref[at, :], preferred_element_type=F32)
        kept_ref[:, : cols // 2] = sums + (kept_ref[:, : cols // 2] if k else 0.0)
    copy.wait()
    kept_ref[:, cols // 2 :] = jnp.dot(scaled_ref[...], other_ref[...], preferred_element_type=F32)
    sent_ref[:rows] = kept_ref[...].astype(BF16)
    across = lax.broadcasted_iota(jnp.int32, (rows, cols), 1)
    down = lax.broadcasted_iota(jnp.int32, (rows, cols), 0)
    total = jnp.sum(jnp.where(across == down, squares_ref[:, :1], 0.0), axis=0, keepdims=True)
    high = total.astype(BF16).astype(F32)
    row = lax.broadcasted_iota(jnp.int32, (16, cols), 0)
    sent_ref[rows:] = jnp.where(row == 0, high, jnp.where(row == 1, total - high, 0.0)).astype(BF16)


def expert(width, info_ref, rows_ref, kept_ref, squares_ref, got_ref, down_ref, out_ref):
    units, half_width = down_ref.shape[0] // 2, down_ref.shape[1]
    which = info_ref[1]
    tail = rows_ref[:, half_width:].astype(F32)
    lane = lax.broadcasted_iota(jnp.int32, tail.shape, 1)
    mine = (lane == which) | (lane == which + EXPERTS)
    weight = jnp.sum(jnp.where(mine, tail, 0.0), axis=1, keepdims=True)
    rows = kept_ref.shape[0]
    far = jnp.sum(got_ref[rows:].astype(F32), axis=0, keepdims=True)
    across = lax.broadcasted_iota(jnp.int32, (rows, far.shape[1]), 1)
    same = across == lax.broadcasted_iota(jnp.int32, (rows, far.shape[1]), 0)
    squares = squares_ref[:, :1] + jnp.sum(jnp.where(same, far, 0.0), axis=1, keepdims=True)
    scale = lax.rsqrt(squares * (1.0 / width) + 1e-06)
    hidden = []
    for at in range(2):
        lo = 2 * units * at
        a = (kept_ref[:, lo : lo + units] + got_ref[:rows, lo : lo + units].astype(F32)) * scale
        lo += units
        b = (kept_ref[:, lo : lo + units] + got_ref[:rows, lo : lo + units].astype(F32)) * scale
        hidden.append((a / (1.0 + jnp.exp(-a)) * b * weight).astype(BF16))
    both = jnp.concatenate(hidden, axis=1)
    deep = half_width // 4
    for k in range(4):
        at = slice(k * deep, (k + 1) * deep)
        out_ref[:, at] = jnp.dot(both, down_ref[:, at], preferred_element_type=F32).astype(BF16)


def gather_parts(back_ref, parts_ref, out_ref):
    out_ref[...] = jnp.dot(back_ref[...], parts_ref[...], preferred_element_type=F32).astype(BF16)


def finish(parts_ref, rows_ref, out_ref, sent_ref):
    half_width = rows_ref.shape[1]
    mixture = parts_ref[0].astype(F32)
    for t in range(1, ALONG):
        mixture += parts_ref[t].astype(F32)
    layer = (rows_ref[...].astype(F32) + mixture).astype(BF16)
    out_ref[...] = layer
    values = layer.astype(F32)
    total = jnp.sum(values * values, axis=1, keepdims=True)
    high = total.astype(BF16).astype(F32)
    lane = lax.broadcasted_iota(jnp.int32, (ROWS, EXTRA), 1)
    pieces = jnp.where(lane == 0, high, jnp.where(lane == 1, total - high, 0.0)).astype(BF16)
    for to in range(sent_ref.shape[0]):
        sent_ref[to, :, :half_width] = layer
        sent_ref[to, :, half_width:] = pieces


def close(width, info_ref, got_ref, gain_ref, out_ref):
    half_width = gain_ref.shape[1]
    values = got_ref[info_ref[2], :, :half_width].astype(F32)
    far = got_ref[info_ref[3], :, half_width:].astype(F32)
    total = jnp.sum(values * values, axis=1, keepdims=True) + jnp.sum(far, axis=1, keepdims=True)
    scale = lax.rsqrt(total * (1.0 / width) + 1e-06)
    out_ref[...] = (values * scale * gain_ref[...].astype(F32)).astype(BF16)


def local(kernel, outs, *args, spaces=None, out_spaces=None, scratch=(), vmem=24 * MIB):
    spaces = spaces or [pltpu.VMEM] * len(args)
    out_spaces = out_spaces or [pltpu.VMEM] * len(outs)
    return pl.pallas_call(
        kernel,
        out_shape=outs,
        in_specs=[pl.BlockSpec(memory_space=space) for space in spaces],
        out_specs=[pl.BlockSpec(memory_space=space) for space in out_spaces],
        scratch_shapes=list(scratch),
        compiler_params=pltpu.CompilerParams(vmem_limit_bytes=vmem),
    )(*args)


def shape(*dims, dtype=BF16):
    return jax.ShapeDtypeStruct(dims, dtype)


def body(section_rows, routes, route_weights, in_gain, gate_up, down, out_gain):
    rows = section_rows[0]
    half_width = rows.shape[1]
    ep = lax.axis_size("ep")
    width = half_width * lax.axis_size("tp")
    units = down.shape[2]
    cols = gate_up.shape[3]
    near, far = crossed_groups(ep, 0), crossed_groups(ep, 1)
    place = lax.axis_index("ep")
    crossed, side = 1 - lax.axis_index("section"), lax.axis_index("tp")
    info = jnp.stack(
        [place % 2, place // SPAN, crossed * 2 + side, crossed * 2 + 1 - side]
    ).astype(jnp.int32)
    other_core = [(i, i ^ 1) for i in range(ep)]
    swap = [(0, 1), (1, 0)]
    full = half_width + EXTRA
    total = ALONG * TIGHT

    gate_own, down_own = gate_up[0, 0], down[0, 0]
    gate_other = lax.ppermute(gate_own, "ep", other_core)
    down_other = lax.ppermute(down_own, "ep", other_core)
    gain_other = lax.ppermute(out_gain, "section", swap)

    down_all = jnp.concatenate([down_own, down_other], axis=0)

    (leaving,) = local(
        announce,
        [shape(ALONG, ROWS, full)],
        rows,
        routes[0],
        route_weights[0],
        spaces=[pltpu.HBM, pltpu.SMEM, pltpu.SMEM],
        out_spaces=[pltpu.HBM],
        scratch=[pltpu.VMEM((ROWS, EXTRA), BF16), pltpu.SemaphoreType.DMA((2 * ALONG,))],
        vmem=60 * MIB,
    )
    met = traded(leaving, near).reshape(WIDE, full)
    sorted_rows, far_back = local(
        sort_rows,
        [shape(total, full), shape(WIDE, total)],
        info,
        met,
        spaces=[pltpu.SMEM, pltpu.VMEM],
        out_spaces=[pltpu.HBM, pltpu.VMEM],
        scratch=[pltpu.VMEM((total, full), BF16), pltpu.SemaphoreType.DMA((-(-full // CHUNK),))],
        vmem=53 * MIB,
    )
    gathered = traded(sorted_rows.reshape(ALONG, TIGHT, full), far).reshape(total, full)
    gathered, gain_other = lax.optimization_barrier((gathered, gain_other))
    kept, sent, squares = local(
        gate,
        [
            shape(total, 2 * cols, dtype=F32),
            shape(total + 16, 2 * cols),
            shape(total, EXTRA, dtype=F32),
        ],
        gathered,
        in_gain,
        gate_own,
        gate_other,
        spaces=[pltpu.VMEM] * 3 + [pl.ANY],
        scratch=[
            pltpu.VMEM((total, half_width), BF16),
            pltpu.VMEM((half_width, cols), BF16),
            pltpu.SemaphoreType.DMA,
        ],
    )
    got = lax.ppermute(sent, "tp", swap)
    (parts,) = local(
        functools.partial(expert, width),
        [shape(total, half_width)],
        info,
        gathered,
        kept,
        squares,
        got,
        down_all,
        spaces=[pltpu.SMEM] + [pltpu.VMEM] * 5,
    )
    returned = traded(parts.reshape(ALONG, TIGHT, half_width), far).reshape(total, half_width)
    (summed,) = local(gather_parts, [shape(WIDE, half_width)], far_back, returned)
    home = traded(summed.reshape(ALONG, ROWS, half_width), near)
    layer_out, leaving = local(
        finish, [shape(ROWS, half_width), shape(4, ROWS, full)], home, rows
    )
    got = lax.all_to_all(leaving, ("section", "tp"), 0, 0, tiled=True)
    (handed,) = local(
        functools.partial(close, width),
        [shape(ROWS, half_width)],
        info,
        got,
        gain_other,
        spaces=[pltpu.SMEM] + [pltpu.VMEM] * 2,
    )
    return (layer_out[None], handed[None])


def solution(mesh):
    return jax.shard_map(
        body,
        mesh=mesh,
        in_specs=(
            P("section", "ep", "tp"),
            P("section", "ep", None),
            P("section", "ep", None),
            P("section", "tp"),
            P("section", "ep", "tp", None),
            P("section", "ep", None, "tp"),
            P("section", "tp"),
        ),
        out_specs=(P("section", "ep", "tp"), P("section", "ep", "tp")),
        check_vma=False,
    )
```

```python
import functools

import jax
import jax.numpy as jnp
from jax import lax
from jax.experimental import pallas as pl
from jax.experimental.pallas import tpu as pltpu
from jax.sharding import PartitionSpec as P

BF16, F32 = jnp.bfloat16, jnp.float32
SPAN = 16
ALONG = 8
ROWS = 4
MOST = 3
EXPERTS = 8
EXTRA = 128
WIDE = ALONG * ROWS
TIGHT = ALONG * MOST
MIB = 1024 * 1024
CHUNK = 1024


def crossed_groups(ep, first):
    along_y = [[y * SPAN + i for y in range(ep // SPAN)] for i in range(SPAN)]
    along_z = [
        [y * SPAN + z * 2 + c for z in range(SPAN // 2)] for y in range(ep // SPAN) for c in range(2)
    ]
    return [g for g in along_z if g[0] % 2 == first] + [g for g in along_y if g[0] % 2 != first]


def traded(block, groups):
    return lax.all_to_all(block, "ep", 0, 0, axis_index_groups=groups, tiled=True)


def index(shape, axis):
    return lax.broadcasted_iota(jnp.int32, shape, axis).astype(F32)


def split(at, count):
    whole = jnp.floor((at + 0.5) * (1.0 / count))
    return whole, at - whole * count


def announce(rows_ref, routes_ref, weights_ref, out_ref):
    half_width = rows_ref.shape[1]
    row = lax.broadcasted_iota(jnp.int32, (ROWS, EXTRA), 0)
    lane = lax.broadcasted_iota(jnp.int32, (ROWS, EXTRA), 1)
    dense = jnp.zeros((ROWS, EXTRA), F32)
    for r in range(ROWS):
        for k in range(routes_ref.shape[1]):
            name = routes_ref[r, k]
            here = (row == r) & ((lane == name) | (lane == name + EXPERTS))
            dense += jnp.where(here, weights_ref[r, k], 0.0)
    high = dense.astype(BF16).astype(F32)
    extra = jnp.where(lane < EXPERTS, high, dense - high).astype(BF16)
    rows = rows_ref[...]
    for t in range(ALONG):
        out_ref[t, :, :half_width] = rows
        out_ref[t, :, half_width:] = extra


def sort_rows(rows_ref, out_ref, back_ref, staged, sems):
    place = lax.axis_index("ep")
    crossing, which = place % 2 == 0, (place // SPAN).astype(F32)
    half_width = rows_ref.shape[1] - EXTRA
    total = ALONG * TIGHT
    tail = rows_ref[:, half_width:].astype(F32)
    named = jnp.where((tail > 0.0) & (index((WIDE, EXTRA), 1) < EXPERTS - 0.5), 1.0, 0.0)
    one, two = index((WIDE, WIDE), 0), index((WIDE, WIDE), 1)
    ahead = jnp.where((split(one, ROWS)[0] == split(two, ROWS)[0]) & (two < one), 1.0, 0.0)
    rank = jnp.dot(ahead.astype(BF16), named.astype(BF16), preferred_element_type=F32)
    code = jnp.where(named > 0.5, rank, -1.0).astype(BF16)

    def matrix(found, at, to):
        source, slot = split(split(at, TIGHT)[1], MOST)
        block = split(to, ROWS)[0]
        return jnp.where((block == source) & (found == slot), 1.0, 0.0).astype(BF16)

    def pick(at, to):
        target = jnp.where(crossing, split(at, TIGHT)[0], which)
        return jnp.where(to == target, 1.0, 0.0).astype(BF16)

    chosen = pick(index((total, 1), 0), index((total, EXTRA), 1))
    found = lax.dot_general(chosen, code, (((1,), (1,)), ((), ())), preferred_element_type=F32)
    forth = matrix(found, index((total, 1), 0), index((1, WIDE), 1))
    copies = []
    for k, lo in enumerate(range(0, half_width + EXTRA, CHUNK)):
        at = pl.ds(lo, min(CHUNK, half_width + EXTRA - lo))
        staged[:, at] = jnp.dot(forth, rows_ref[:, at], preferred_element_type=F32).astype(BF16)
        copies.append(pltpu.make_async_copy(staged.at[:, at], out_ref.at[:, at], sems.at[k]))
        copies[k].start()
    chosen = pick(index((1, total), 1), index((EXTRA, total), 0))
    found = jnp.dot(code, chosen, preferred_element_type=F32)
    back_ref[...] = matrix(found, index((1, total), 1), index((WIDE, 1), 0))
    for copy in copies:
        copy.wait()


def gate(
    rows_ref, gain_ref, own_ref, other_hbm, kept_ref, sent_ref, squares_ref, scaled_ref, other_ref, sem
):
    copy = pltpu.make_async_copy(other_hbm, other_ref, sem)
    copy.start()
    half_width, cols = own_ref.shape[0], kept_ref.shape[1]
    rows = rows_ref.shape[0]
    deep = half_width // 7
    for k in range(7):
        at = slice(k * deep, (k + 1) * deep)
        values = rows_ref[:, at].astype(F32)
        part = jnp.sum(values * values, axis=1, keepdims=True)
        squares_ref[...] = jnp.broadcast_to(part, squares_ref.shape) + (
            squares_ref[...] if k else 0.0
        )
        scaled = (values * gain_ref[:, at].astype(F32)).astype(BF16)
        scaled_ref[:, at] = scaled
        sums = jnp.dot(scaled, own_ref[at, :], preferred_element_type=F32)
        kept_ref[:, : cols // 2] = sums + (kept_ref[:, : cols // 2] if k else 0.0)
    copy.wait()
    kept_ref[:, cols // 2 :] = jnp.dot(scaled_ref[...], other_ref[...], preferred_element_type=F32)
    sent_ref[:rows] = kept_ref[...].astype(BF16)
    across = lax.broadcasted_iota(jnp.int32, (rows, cols), 1)
    down = lax.broadcasted_iota(jnp.int32, (rows, cols), 0)
    total = jnp.sum(jnp.where(across == down, squares_ref[:, :1], 0.0), axis=0, keepdims=True)
    high = total.astype(BF16).astype(F32)
    row = lax.broadcasted_iota(jnp.int32, (16, cols), 0)
    sent_ref[rows:] = jnp.where(row == 0, high, jnp.where(row == 1, total - high, 0.0)).astype(BF16)


def expert(width, rows_ref, kept_ref, squares_ref, got_ref, down_ref, out_ref):
    units, half_width = down_ref.shape[0] // 2, down_ref.shape[1]
    which = lax.axis_index("ep") // SPAN
    tail = rows_ref[:, half_width:].astype(F32)
    lane = lax.broadcasted_iota(jnp.int32, tail.shape, 1)
    mine = (lane == which) | (lane == which + EXPERTS)
    weight = jnp.sum(jnp.where(mine, tail, 0.0), axis=1, keepdims=True)
    rows = kept_ref.shape[0]
    far = jnp.sum(got_ref[rows:].astype(F32), axis=0, keepdims=True)
    across = lax.broadcasted_iota(jnp.int32, (rows, far.shape[1]), 1)
    same = across == lax.broadcasted_iota(jnp.int32, (rows, far.shape[1]), 0)
    squares = squares_ref[:, :1] + jnp.sum(jnp.where(same, far, 0.0), axis=1, keepdims=True)
    scale = lax.rsqrt(squares * (1.0 / width) + 1e-06)
    hidden = []
    for at in range(2):
        lo = 2 * units * at
        a = (kept_ref[:, lo : lo + units] + got_ref[:rows, lo : lo + units].astype(F32)) * scale
        lo += units
        b = (kept_ref[:, lo : lo + units] + got_ref[:rows, lo : lo + units].astype(F32)) * scale
        hidden.append((a / (1.0 + jnp.exp(-a)) * b * weight).astype(BF16))
    both = jnp.concatenate(hidden, axis=1)
    deep = half_width // 4
    for k in range(4):
        at = slice(k * deep, (k + 1) * deep)
        out_ref[:, at] = jnp.dot(both, down_ref[:, at], preferred_element_type=F32).astype(BF16)


def gather_parts(back_ref, parts_ref, out_ref):
    out_ref[...] = jnp.dot(back_ref[...], parts_ref[...], preferred_element_type=F32).astype(BF16)


def finish(parts_ref, rows_ref, out_ref, sent_ref):
    half_width = rows_ref.shape[1]
    mixture = parts_ref[0].astype(F32)
    for t in range(1, ALONG):
        mixture += parts_ref[t].astype(F32)
    layer = (rows_ref[...].astype(F32) + mixture).astype(BF16)
    out_ref[...] = layer
    values = layer.astype(F32)
    total = jnp.sum(values * values, axis=1, keepdims=True)
    high = total.astype(BF16).astype(F32)
    lane = lax.broadcasted_iota(jnp.int32, (ROWS, EXTRA), 1)
    pieces = jnp.where(lane == 0, high, jnp.where(lane == 1, total - high, 0.0)).astype(BF16)
    for to in range(sent_ref.shape[0]):
        sent_ref[to, :, :half_width] = layer
        sent_ref[to, :, half_width:] = pieces


def close(width, got_ref, gain_ref, out_ref):
    half_width = gain_ref.shape[1]
    crossed, side = 1 - lax.axis_index("section"), lax.axis_index("tp")
    values = got_ref[crossed * 2 + side, :, :half_width].astype(F32)
    far = got_ref[crossed * 2 + 1 - side, :, half_width:].astype(F32)
    total = jnp.sum(values * values, axis=1, keepdims=True) + jnp.sum(far, axis=1, keepdims=True)
    scale = lax.rsqrt(total * (1.0 / width) + 1e-06)
    out_ref[...] = (values * scale * gain_ref[...].astype(F32)).astype(BF16)


def local(kernel, outs, *args, spaces=None, out_spaces=None, scratch=(), vmem=24 * MIB):
    spaces = spaces or [pltpu.VMEM] * len(args)
    out_spaces = out_spaces or [pltpu.VMEM] * len(outs)
    return pl.pallas_call(
        kernel,
        out_shape=outs,
        in_specs=[pl.BlockSpec(memory_space=space) for space in spaces],
        out_specs=[pl.BlockSpec(memory_space=space) for space in out_spaces],
        scratch_shapes=list(scratch),
        compiler_params=pltpu.CompilerParams(vmem_limit_bytes=vmem),
    )(*args)


def shape(*dims, dtype=BF16):
    return jax.ShapeDtypeStruct(dims, dtype)


def body(section_rows, routes, route_weights, in_gain, gate_up, down, out_gain):
    rows = section_rows[0]
    half_width = rows.shape[1]
    ep = lax.axis_size("ep")
    width = half_width * lax.axis_size("tp")
    units = down.shape[2]
    cols = gate_up.shape[3]
    near, far = crossed_groups(ep, 0), crossed_groups(ep, 1)
    other_core = [(i, i ^ 1) for i in range(ep)]
    swap = [(0, 1), (1, 0)]
    full = half_width + EXTRA
    total = ALONG * TIGHT

    gate_own, down_own = gate_up[0, 0], down[0, 0]
    gate_other = lax.ppermute(gate_own, "ep", other_core)
    down_other = lax.ppermute(down_own, "ep", other_core)
    gain_other = lax.ppermute(out_gain, "section", swap)

    down_all = jnp.concatenate([down_own, down_other], axis=0)

    (leaving,) = local(
        announce,
        [shape(ALONG, ROWS, full)],
        rows,
        routes[0],
        route_weights[0],
        spaces=[pltpu.VMEM, pltpu.SMEM, pltpu.SMEM],
        vmem=60 * MIB,
    )
    met = traded(leaving, near).reshape(WIDE, full)
    sorted_rows, far_back = local(
        sort_rows,
        [shape(total, full), shape(WIDE, total)],
        met,
        out_spaces=[pltpu.HBM, pltpu.VMEM],
        scratch=[pltpu.VMEM((total, full), BF16), pltpu.SemaphoreType.DMA((-(-full // CHUNK),))],
        vmem=53 * MIB,
    )
    gathered = traded(sorted_rows.reshape(ALONG, TIGHT, full), far).reshape(total, full)
    gathered, gain_other = lax.optimization_barrier((gathered, gain_other))
    kept, sent, squares = local(
        gate,
        [
            shape(total, 2 * cols, dtype=F32),
            shape(total + 16, 2 * cols),
            shape(total, EXTRA, dtype=F32),
        ],
        gathered,
        in_gain,
        gate_own,
        gate_other,
        spaces=[pltpu.VMEM] * 3 + [pl.ANY],
        scratch=[
            pltpu.VMEM((total, half_width), BF16),
            pltpu.VMEM((half_width, cols), BF16),
            pltpu.SemaphoreType.DMA,
        ],
    )
    got = lax.ppermute(sent, "tp", swap)
    (parts,) = local(
        functools.partial(expert, width),
        [shape(total, half_width)],
        gathered,
        kept,
        squares,
        got,
        down_all,
    )
    returned = traded(parts.reshape(ALONG, TIGHT, half_width), far).reshape(total, half_width)
    (summed,) = local(gather_parts, [shape(WIDE, half_width)], far_back, returned)
    home = traded(summed.reshape(ALONG, ROWS, half_width), near)
    layer_out, leaving = local(
        finish, [shape(ROWS, half_width), shape(4, ROWS, full)], home, rows
    )
    got = lax.all_to_all(leaving, ("section", "tp"), 0, 0, tiled=True)
    (handed,) = local(
        functools.partial(close, width),
        [shape(ROWS, half_width)],
        got,
        gain_other,
    )
    return (layer_out[None], handed[None])


def solution(mesh):
    return jax.shard_map(
        body,
        mesh=mesh,
        in_specs=(
            P("section", "ep", "tp"),
            P("section", "ep", None),
            P("section", "ep", None),
            P("section", "tp"),
            P("section", "ep", "tp", None),
            P("section", "ep", None, "tp"),
            P("section", "tp"),
        ),
        out_specs=(P("section", "ep", "tp"), P("section", "ep", "tp")),
        check_vma=False,
    )
```

```python
import functools

import jax
import jax.numpy as jnp
from jax import lax
from jax.experimental import pallas as pl
from jax.experimental.pallas import tpu as pltpu
from jax.sharding import PartitionSpec as P

BF16, F32 = jnp.bfloat16, jnp.float32
SPAN = 16
ALONG = 8
ROWS = 4
MOST = 3
EXPERTS = 8
EXTRA = 128
WIDE = ALONG * ROWS
TIGHT = ALONG * MOST
MIB = 1024 * 1024
CHUNK = 1024


def crossed_groups(ep, first):
    along_y = [[y * SPAN + i for y in range(ep // SPAN)] for i in range(SPAN)]
    along_z = [
        [y * SPAN + z * 2 + c for z in range(SPAN // 2)] for y in range(ep // SPAN) for c in range(2)
    ]
    return [g for g in along_z if g[0] % 2 == first] + [g for g in along_y if g[0] % 2 != first]


def traded(block, groups):
    return lax.all_to_all(block, "ep", 0, 0, axis_index_groups=groups, tiled=True)


def index(shape, axis):
    return lax.broadcasted_iota(jnp.int32, shape, axis).astype(F32)


def split(at, count):
    whole = jnp.floor((at + 0.5) * (1.0 / count))
    return whole, at - whole * count


def announce(rows_ref, routes_ref, weights_ref, out_ref):
    half_width = rows_ref.shape[1]
    lane = lax.broadcasted_iota(jnp.int32, (ROWS, EXTRA), 1)
    dense = jnp.zeros((ROWS, EXTRA), F32)
    routes, weights = routes_ref[...], weights_ref[...]
    for k in range(routes.shape[1]):
        name = routes[:, k : k + 1]
        dense += jnp.where((lane == name) | (lane == name + EXPERTS), weights[:, k : k + 1], 0.0)
    high = dense.astype(BF16).astype(F32)
    extra = jnp.where(lane < EXPERTS, high, dense - high).astype(BF16)
    rows = rows_ref[...]
    for t in range(ALONG):
        out_ref[t, :, :half_width] = rows
        out_ref[t, :, half_width:] = extra


def sort_rows(rows_ref, out_ref, back_ref, staged, sems):
    place = lax.axis_index("ep")
    crossing, which = place % 2 == 1, (place // SPAN).astype(F32)
    half_width = rows_ref.shape[1] - EXTRA
    total = ALONG * TIGHT
    tail = rows_ref[:, half_width:].astype(F32)
    named = jnp.where((tail > 0.0) & (index((WIDE, EXTRA), 1) < EXPERTS - 0.5), 1.0, 0.0)
    one, two = index((WIDE, WIDE), 0), index((WIDE, WIDE), 1)
    ahead = jnp.where((split(one, ROWS)[0] == split(two, ROWS)[0]) & (two < one), 1.0, 0.0)
    rank = jnp.dot(ahead.astype(BF16), named.astype(BF16), preferred_element_type=F32)
    code = jnp.where(named > 0.5, rank, -1.0).astype(BF16)

    def matrix(found, at, to):
        source, slot = split(split(at, TIGHT)[1], MOST)
        block = split(to, ROWS)[0]
        return jnp.where((block == source) & (found == slot), 1.0, 0.0).astype(BF16)

    def pick(at, to):
        target = jnp.where(crossing, split(at, TIGHT)[0], which)
        return jnp.where(to == target, 1.0, 0.0).astype(BF16)

    chosen = pick(index((total, 1), 0), index((total, EXTRA), 1))
    found = lax.dot_general(chosen, code, (((1,), (1,)), ((), ())), preferred_element_type=F32)
    forth = matrix(found, index((total, 1), 0), index((1, WIDE), 1))
    copies = []
    for k, lo in enumerate(range(0, half_width + EXTRA, CHUNK)):
        at = pl.ds(lo, min(CHUNK, half_width + EXTRA - lo))
        staged[:, at] = jnp.dot(forth, rows_ref[:, at], preferred_element_type=F32).astype(BF16)
        copies.append(pltpu.make_async_copy(staged.at[:, at], out_ref.at[:, at], sems.at[k]))
        copies[k].start()
    chosen = pick(index((1, total), 1), index((EXTRA, total), 0))
    found = jnp.dot(code, chosen, preferred_element_type=F32)
    back_ref[...] = matrix(found, index((1, total), 1), index((WIDE, 1), 0))
    for copy in copies:
        copy.wait()


def gate(
    rows_ref, gain_ref, own_ref, other_hbm, kept_ref, sent_ref, squares_ref, scaled_ref, other_ref, sem
):
    copy = pltpu.make_async_copy(other_hbm, other_ref, sem)
    copy.start()
    half_width, cols = own_ref.shape[0], kept_ref.shape[1]
    rows = rows_ref.shape[0]
    deep = half_width // 7
    for k in range(7):
        at = slice(k * deep, (k + 1) * deep)
        values = rows_ref[:, at].astype(F32)
        part = jnp.sum(values * values, axis=1, keepdims=True)
        squares_ref[...] = jnp.broadcast_to(part, squares_ref.shape) + (
            squares_ref[...] if k else 0.0
        )
        scaled = (values * gain_ref[:, at].astype(F32)).astype(BF16)
        scaled_ref[:, at] = scaled
        sums = jnp.dot(scaled, own_ref[at, :], preferred_element_type=F32)
        kept_ref[:, : cols // 2] = sums + (kept_ref[:, : cols // 2] if k else 0.0)
    copy.wait()
    kept_ref[:, cols // 2 :] = jnp.dot(scaled_ref[...], other_ref[...], preferred_element_type=F32)
    sent_ref[:rows] = kept_ref[...].astype(BF16)
    across = lax.broadcasted_iota(jnp.int32, (rows, cols), 1)
    down = lax.broadcasted_iota(jnp.int32, (rows, cols), 0)
    total = jnp.sum(jnp.where(across == down, squares_ref[:, :1], 0.0), axis=0, keepdims=True)
    high = total.astype(BF16).astype(F32)
    row = lax.broadcasted_iota(jnp.int32, (16, cols), 0)
    sent_ref[rows:] = jnp.where(row == 0, high, jnp.where(row == 1, total - high, 0.0)).astype(BF16)


def expert(width, rows_ref, kept_ref, squares_ref, got_ref, down_ref, out_ref):
    units, half_width = down_ref.shape[0] // 2, down_ref.shape[1]
    which = lax.axis_index("ep") // SPAN
    tail = rows_ref[:, half_width:].astype(F32)
    lane = lax.broadcasted_iota(jnp.int32, tail.shape, 1)
    mine = (lane == which) | (lane == which + EXPERTS)
    weight = jnp.sum(jnp.where(mine, tail, 0.0), axis=1, keepdims=True)
    rows = kept_ref.shape[0]
    far = jnp.sum(got_ref[rows:].astype(F32), axis=0, keepdims=True)
    across = lax.broadcasted_iota(jnp.int32, (rows, far.shape[1]), 1)
    same = across == lax.broadcasted_iota(jnp.int32, (rows, far.shape[1]), 0)
    squares = squares_ref[:, :1] + jnp.sum(jnp.where(same, far, 0.0), axis=1, keepdims=True)
    scale = lax.rsqrt(squares * (1.0 / width) + 1e-06)
    hidden = []
    for at in range(2):
        lo = 2 * units * at
        a = (kept_ref[:, lo : lo + units] + got_ref[:rows, lo : lo + units].astype(F32)) * scale
        lo += units
        b = (kept_ref[:, lo : lo + units] + got_ref[:rows, lo : lo + units].astype(F32)) * scale
        hidden.append((a / (1.0 + jnp.exp(-a)) * b * weight).astype(BF16))
    both = jnp.concatenate(hidden, axis=1)
    deep = half_width // 4
    for k in range(4):
        at = slice(k * deep, (k + 1) * deep)
        out_ref[:, at] = jnp.dot(both, down_ref[:, at], preferred_element_type=F32).astype(BF16)


def gather_parts(back_ref, parts_ref, out_ref):
    out_ref[...] = jnp.dot(back_ref[...], parts_ref[...], preferred_element_type=F32).astype(BF16)


def finish(parts_ref, rows_ref, out_ref, sent_ref):
    half_width = rows_ref.shape[1]
    mixture = parts_ref[0].astype(F32)
    for t in range(1, ALONG):
        mixture += parts_ref[t].astype(F32)
    layer = (rows_ref[...].astype(F32) + mixture).astype(BF16)
    out_ref[...] = layer
    values = layer.astype(F32)
    total = jnp.sum(values * values, axis=1, keepdims=True)
    high = total.astype(BF16).astype(F32)
    lane = lax.broadcasted_iota(jnp.int32, (ROWS, EXTRA), 1)
    pieces = jnp.where(lane == 0, high, jnp.where(lane == 1, total - high, 0.0)).astype(BF16)
    for to in range(sent_ref.shape[0]):
        sent_ref[to, :, :half_width] = layer
        sent_ref[to, :, half_width:] = pieces


def close(width, got_ref, gain_ref, out_ref):
    half_width = gain_ref.shape[1]
    crossed, side = 1 - lax.axis_index("section"), lax.axis_index("tp")
    values = got_ref[crossed * 2 + side, :, :half_width].astype(F32)
    far = got_ref[crossed * 2 + 1 - side, :, half_width:].astype(F32)
    total = jnp.sum(values * values, axis=1, keepdims=True) + jnp.sum(far, axis=1, keepdims=True)
    scale = lax.rsqrt(total * (1.0 / width) + 1e-06)
    out_ref[...] = (values * scale * gain_ref[...].astype(F32)).astype(BF16)


def local(kernel, outs, *args, spaces=None, out_spaces=None, scratch=(), vmem=24 * MIB):
    spaces = spaces or [pltpu.VMEM] * len(args)
    out_spaces = out_spaces or [pltpu.VMEM] * len(outs)
    return pl.pallas_call(
        kernel,
        out_shape=outs,
        in_specs=[pl.BlockSpec(memory_space=space) for space in spaces],
        out_specs=[pl.BlockSpec(memory_space=space) for space in out_spaces],
        scratch_shapes=list(scratch),
        compiler_params=pltpu.CompilerParams(vmem_limit_bytes=vmem),
    )(*args)


def shape(*dims, dtype=BF16):
    return jax.ShapeDtypeStruct(dims, dtype)


def body(section_rows, routes, route_weights, in_gain, gate_up, down, out_gain):
    rows = section_rows[0]
    half_width = rows.shape[1]
    ep = lax.axis_size("ep")
    width = half_width * lax.axis_size("tp")
    units = down.shape[2]
    cols = gate_up.shape[3]
    near, far = crossed_groups(ep, 1), crossed_groups(ep, 0)
    other_core = [(i, i ^ 1) for i in range(ep)]
    swap = [(0, 1), (1, 0)]
    full = half_width + EXTRA
    total = ALONG * TIGHT

    gate_own, down_own = gate_up[0, 0], down[0, 0]
    gate_other = lax.ppermute(gate_own, "ep", other_core)
    down_other = lax.ppermute(down_own, "ep", other_core)
    gain_other = lax.ppermute(out_gain, "section", swap)

    down_all = jnp.concatenate([down_own, down_other], axis=0)

    (leaving,) = local(
        announce,
        [shape(ALONG, ROWS, full)],
        rows,
        routes[0],
        route_weights[0],
        vmem=60 * MIB,
    )
    met = traded(leaving, near).reshape(WIDE, full)
    sorted_rows, far_back = local(
        sort_rows,
        [shape(total, full), shape(WIDE, total)],
        met,
        out_spaces=[pltpu.HBM, pltpu.VMEM],
        scratch=[pltpu.VMEM((total, full), BF16), pltpu.SemaphoreType.DMA((-(-full // CHUNK),))],
        vmem=53 * MIB,
    )
    gathered = traded(sorted_rows.reshape(ALONG, TIGHT, full), far).reshape(total, full)
    gathered, gain_other = lax.optimization_barrier((gathered, gain_other))
    kept, sent, squares = local(
        gate,
        [
            shape(total, 2 * cols, dtype=F32),
            shape(total + 16, 2 * cols),
            shape(total, EXTRA, dtype=F32),
        ],
        gathered,
        in_gain,
        gate_own,
        gate_other,
        spaces=[pltpu.VMEM] * 3 + [pl.ANY],
        scratch=[
            pltpu.VMEM((total, half_width), BF16),
            pltpu.VMEM((half_width, cols), BF16),
            pltpu.SemaphoreType.DMA,
        ],
    )
    got = lax.ppermute(sent, "tp", swap)
    (parts,) = local(
        functools.partial(expert, width),
        [shape(total, half_width)],
        gathered,
        kept,
        squares,
        got,
        down_all,
    )
    returned = traded(parts.reshape(ALONG, TIGHT, half_width), far).reshape(total, half_width)
    (summed,) = local(gather_parts, [shape(WIDE, half_width)], far_back, returned)
    home = traded(summed.reshape(ALONG, ROWS, half_width), near)
    layer_out, leaving = local(
        finish, [shape(ROWS, half_width), shape(4, ROWS, full)], home, rows
    )
    got = lax.all_to_all(leaving, ("section", "tp"), 0, 0, tiled=True)
    (handed,) = local(
        functools.partial(close, width),
        [shape(ROWS, half_width)],
        got,
        gain_other,
    )
    return (layer_out[None], handed[None])


def solution(mesh):
    return jax.shard_map(
        body,
        mesh=mesh,
        in_specs=(
            P("section", "ep", "tp"),
            P("section", "ep", None),
            P("section", "ep", None),
            P("section", "tp"),
            P("section", "ep", "tp", None),
            P("section", "ep", None, "tp"),
            P("section", "tp"),
        ),
        out_specs=(P("section", "ep", "tp"), P("section", "ep", "tp")),
        check_vma=False,
    )
```

```python
import functools

import jax
import jax.numpy as jnp
from jax import lax
from jax.experimental import pallas as pl
from jax.experimental.pallas import tpu as pltpu
from jax.sharding import PartitionSpec as P

BF16, F32 = jnp.bfloat16, jnp.float32
SPAN = 16
ALONG = 8
ROWS = 4
MOST = 3
EXPERTS = 8
EXTRA = 128
WIDE = ALONG * ROWS
TIGHT = ALONG * MOST
MIB = 1024 * 1024
CHUNK = 1024


def crossed_groups(ep, first):
    along_y = [[y * SPAN + i for y in range(ep // SPAN)] for i in range(SPAN)]
    along_z = [
        [y * SPAN + z * 2 + c for z in range(SPAN // 2)] for y in range(ep // SPAN) for c in range(2)
    ]
    return [g for g in along_z if g[0] % 2 == first] + [g for g in along_y if g[0] % 2 != first]


def traded(block, groups):
    return lax.all_to_all(block, "ep", 0, 0, axis_index_groups=groups, tiled=True)


def index(shape, axis):
    return lax.broadcasted_iota(jnp.int32, shape, axis).astype(F32)


def split(at, count):
    whole = jnp.floor((at + 0.5) * (1.0 / count))
    return whole, at - whole * count


def announce(rows_ref, routes_ref, weights_ref, out_ref):
    half_width = rows_ref.shape[1]
    lane = lax.broadcasted_iota(jnp.int32, (ROWS, EXTRA), 1)
    dense = jnp.zeros((ROWS, EXTRA), F32)
    routes, weights = routes_ref[...], weights_ref[...]
    for k in range(routes.shape[1]):
        name = routes[:, k : k + 1]
        dense += jnp.where((lane == name) | (lane == name + EXPERTS), weights[:, k : k + 1], 0.0)
    high = dense.astype(BF16).astype(F32)
    extra = jnp.where(lane < EXPERTS, high, dense - high).astype(BF16)
    rows = rows_ref[...]
    for t in range(ALONG):
        out_ref[t, :, :half_width] = rows
        out_ref[t, :, half_width:] = extra


def sort_rows(rows_ref, out_ref, back_ref, staged, sems):
    place = lax.axis_index("ep")
    crossing, which = place % 2 == 1, (place // SPAN).astype(F32)
    half_width = rows_ref.shape[1] - EXTRA
    total = ALONG * TIGHT
    tail = rows_ref[:, half_width:].astype(F32)
    named = jnp.where((tail > 0.0) & (index((WIDE, EXTRA), 1) < EXPERTS - 0.5), 1.0, 0.0)
    one, two = index((WIDE, WIDE), 0), index((WIDE, WIDE), 1)
    ahead = jnp.where((split(one, ROWS)[0] == split(two, ROWS)[0]) & (two < one), 1.0, 0.0)
    rank = jnp.dot(ahead.astype(BF16), named.astype(BF16), preferred_element_type=F32)
    code = jnp.where(named > 0.5, rank, -1.0).astype(BF16)

    def matrix(found, at, to):
        source, slot = split(split(at, TIGHT)[1], MOST)
        block = split(to, ROWS)[0]
        return jnp.where((block == source) & (found == slot), 1.0, 0.0).astype(BF16)

    def pick(at, to):
        target = jnp.where(crossing, split(at, TIGHT)[0], which)
        return jnp.where(to == target, 1.0, 0.0).astype(BF16)

    chosen = pick(index((total, 1), 0), index((total, EXTRA), 1))
    found = lax.dot_general(chosen, code, (((1,), (1,)), ((), ())), preferred_element_type=F32)
    forth = matrix(found, index((total, 1), 0), index((1, WIDE), 1))
    copies = []
    for k, lo in enumerate(range(0, half_width + EXTRA, CHUNK)):
        at = pl.ds(lo, min(CHUNK, half_width + EXTRA - lo))
        staged[:, at] = jnp.dot(forth, rows_ref[:, at], preferred_element_type=F32).astype(BF16)
        copies.append(pltpu.make_async_copy(staged.at[:, at], out_ref.at[:, at], sems.at[k]))
        copies[k].start()
    chosen = pick(index((1, total), 1), index((EXTRA, total), 0))
    found = jnp.dot(code, chosen, preferred_element_type=F32)
    back_ref[...] = matrix(found, index((1, total), 1), index((WIDE, 1), 0))
    for copy in copies:
        copy.wait()


def gate(
    rows_ref, gain_ref, own_ref, other_hbm, kept_ref, sent_ref, squares_ref, scaled_ref, other_ref, sem
):
    copy = pltpu.make_async_copy(other_hbm, other_ref, sem)
    copy.start()
    half_width, cols = own_ref.shape[0], kept_ref.shape[1]
    rows = rows_ref.shape[0]
    deep = half_width // 7
    for k in range(7):
        at = slice(k * deep, (k + 1) * deep)
        values = rows_ref[:, at].astype(F32)
        for lo in range(0, deep, EXTRA):
            piece = values[:, lo : lo + EXTRA]
            squares = piece * piece + (squares if k or lo else 0.0)
        scaled = (values * gain_ref[:, at].astype(F32)).astype(BF16)
        scaled_ref[:, at] = scaled
        sums = jnp.dot(scaled, own_ref[at, :], preferred_element_type=F32)
        kept_ref[:, : cols // 2] = sums + (kept_ref[:, : cols // 2] if k else 0.0)
    copy.wait()
    kept_ref[:, cols // 2 :] = jnp.dot(scaled_ref[...], other_ref[...], preferred_element_type=F32)
    squares = jnp.sum(squares, axis=1, keepdims=True)
    squares_ref[...] = jnp.broadcast_to(squares, squares_ref.shape)
    sent_ref[:rows] = kept_ref[...].astype(BF16)
    across = lax.broadcasted_iota(jnp.int32, (rows, cols), 1)
    down = lax.broadcasted_iota(jnp.int32, (rows, cols), 0)
    total = jnp.sum(jnp.where(across == down, squares, 0.0), axis=0, keepdims=True)
    high = total.astype(BF16).astype(F32)
    row = lax.broadcasted_iota(jnp.int32, (16, cols), 0)
    sent_ref[rows:] = jnp.where(row == 0, high, jnp.where(row == 1, total - high, 0.0)).astype(BF16)


def expert(width, rows_ref, kept_ref, squares_ref, got_ref, down_ref, out_ref):
    units, half_width = down_ref.shape[0] // 2, down_ref.shape[1]
    which = lax.axis_index("ep") // SPAN
    tail = rows_ref[:, half_width:].astype(F32)
    lane = lax.broadcasted_iota(jnp.int32, tail.shape, 1)
    mine = (lane == which) | (lane == which + EXPERTS)
    weight = jnp.sum(jnp.where(mine, tail, 0.0), axis=1, keepdims=True)
    rows = kept_ref.shape[0]
    far = jnp.sum(got_ref[rows:].astype(F32), axis=0, keepdims=True)
    across = lax.broadcasted_iota(jnp.int32, (rows, far.shape[1]), 1)
    same = across == lax.broadcasted_iota(jnp.int32, (rows, far.shape[1]), 0)
    squares = squares_ref[:, :1] + jnp.sum(jnp.where(same, far, 0.0), axis=1, keepdims=True)
    scale = lax.rsqrt(squares * (1.0 / width) + 1e-06)
    hidden = []
    for at in range(2):
        lo = 2 * units * at
        a = (kept_ref[:, lo : lo + units] + got_ref[:rows, lo : lo + units].astype(F32)) * scale
        lo += units
        b = (kept_ref[:, lo : lo + units] + got_ref[:rows, lo : lo + units].astype(F32)) * scale
        hidden.append((a / (1.0 + jnp.exp(-a)) * b * weight).astype(BF16))
    both = jnp.concatenate(hidden, axis=1)
    deep = half_width // 4
    for k in range(4):
        at = slice(k * deep, (k + 1) * deep)
        out_ref[:, at] = jnp.dot(both, down_ref[:, at], preferred_element_type=F32).astype(BF16)


def gather_parts(back_ref, parts_ref, out_ref):
    sums = jnp.dot(back_ref[...], parts_ref[...], preferred_element_type=F32).astype(BF16)
    for t in range(ALONG):
        out_ref[t] = sums[t * ROWS : (t + 1) * ROWS]


def finish(parts_ref, rows_ref, out_ref, sent_ref):
    half_width = rows_ref.shape[1]
    mixture = parts_ref[0].astype(F32)
    for t in range(1, ALONG):
        mixture += parts_ref[t].astype(F32)
    layer = (rows_ref[...].astype(F32) + mixture).astype(BF16)
    out_ref[...] = layer
    values = layer.astype(F32)
    total = jnp.sum(values * values, axis=1, keepdims=True)
    high = total.astype(BF16).astype(F32)
    lane = lax.broadcasted_iota(jnp.int32, (ROWS, EXTRA), 1)
    pieces = jnp.where(lane == 0, high, jnp.where(lane == 1, total - high, 0.0)).astype(BF16)
    for to in range(sent_ref.shape[0]):
        sent_ref[to, :, :half_width] = layer
        sent_ref[to, :, half_width:] = pieces


def close(width, got_ref, gain_ref, out_ref):
    half_width = gain_ref.shape[1]
    crossed, side = 1 - lax.axis_index("section"), lax.axis_index("tp")
    values = got_ref[crossed * 2 + side, :, :half_width].astype(F32)
    far = got_ref[crossed * 2 + 1 - side, :, half_width:].astype(F32)
    total = jnp.sum(values * values, axis=1, keepdims=True) + jnp.sum(far, axis=1, keepdims=True)
    scale = lax.rsqrt(total * (1.0 / width) + 1e-06)
    out_ref[...] = (values * scale * gain_ref[...].astype(F32)).astype(BF16)


def local(kernel, outs, *args, spaces=None, out_spaces=None, scratch=(), vmem=24 * MIB):
    spaces = spaces or [pltpu.VMEM] * len(args)
    out_spaces = out_spaces or [pltpu.VMEM] * len(outs)
    return pl.pallas_call(
        kernel,
        out_shape=outs,
        in_specs=[pl.BlockSpec(memory_space=space) for space in spaces],
        out_specs=[pl.BlockSpec(memory_space=space) for space in out_spaces],
        scratch_shapes=list(scratch),
        compiler_params=pltpu.CompilerParams(vmem_limit_bytes=vmem),
    )(*args)


def shape(*dims, dtype=BF16):
    return jax.ShapeDtypeStruct(dims, dtype)


def body(section_rows, routes, route_weights, in_gain, gate_up, down, out_gain):
    rows = section_rows[0]
    half_width = rows.shape[1]
    ep = lax.axis_size("ep")
    width = half_width * lax.axis_size("tp")
    units = down.shape[2]
    cols = gate_up.shape[3]
    near, far = crossed_groups(ep, 1), crossed_groups(ep, 0)
    other_core = [(i, i ^ 1) for i in range(ep)]
    swap = [(0, 1), (1, 0)]
    full = half_width + EXTRA
    total = ALONG * TIGHT

    gate_own, down_own = gate_up[0, 0], down[0, 0]
    gate_other = lax.ppermute(gate_own, "ep", other_core)
    down_other = lax.ppermute(down_own, "ep", other_core)
    gain_other = lax.ppermute(out_gain, "section", swap)

    down_all = jnp.concatenate([down_own, down_other], axis=0)

    (leaving,) = local(
        announce,
        [shape(ALONG, ROWS, full)],
        rows,
        routes[0],
        route_weights[0],
        vmem=60 * MIB,
    )
    met = traded(leaving, near).reshape(WIDE, full)
    sorted_rows, far_back = local(
        sort_rows,
        [shape(total, full), shape(WIDE, total)],
        met,
        out_spaces=[pltpu.HBM, pltpu.VMEM],
        scratch=[pltpu.VMEM((total, full), BF16), pltpu.SemaphoreType.DMA((-(-full // CHUNK),))],
        vmem=53 * MIB,
    )
    gathered = traded(sorted_rows.reshape(ALONG, TIGHT, full), far).reshape(total, full)
    gathered, gain_other = lax.optimization_barrier((gathered, gain_other))
    kept, sent, squares = local(
        gate,
        [
            shape(total, 2 * cols, dtype=F32),
            shape(total + 16, 2 * cols),
            shape(total, EXTRA, dtype=F32),
        ],
        gathered,
        in_gain,
        gate_own,
        gate_other,
        spaces=[pltpu.VMEM] * 3 + [pl.ANY],
        scratch=[
            pltpu.VMEM((total, half_width), BF16),
            pltpu.VMEM((half_width, cols), BF16),
            pltpu.SemaphoreType.DMA,
        ],
    )
    got = lax.ppermute(sent, "tp", swap)
    (parts,) = local(
        functools.partial(expert, width),
        [shape(total, half_width)],
        gathered,
        kept,
        squares,
        got,
        down_all,
    )
    returned = traded(parts.reshape(ALONG, TIGHT, half_width), far).reshape(total, half_width)
    (summed,) = local(gather_parts, [shape(ALONG, ROWS, half_width)], far_back, returned)
    home = traded(summed, near)
    layer_out, leaving = local(
        finish, [shape(ROWS, half_width), shape(4, ROWS, full)], home, rows
    )
    got = lax.all_to_all(leaving, ("section", "tp"), 0, 0, tiled=True)
    (handed,) = local(
        functools.partial(close, width),
        [shape(ROWS, half_width)],
        got,
        gain_other,
    )
    return (layer_out[None], handed[None])


def solution(mesh):
    return jax.shard_map(
        body,
        mesh=mesh,
        in_specs=(
            P("section", "ep", "tp"),
            P("section", "ep", None),
            P("section", "ep", None),
            P("section", "tp"),
            P("section", "ep", "tp", None),
            P("section", "ep", None, "tp"),
            P("section", "tp"),
        ),
        out_specs=(P("section", "ep", "tp"), P("section", "ep", "tp")),
        check_vma=False,
    )
```

```python
import functools

import jax
import jax.numpy as jnp
from jax import lax
from jax.experimental import pallas as pl
from jax.experimental.pallas import tpu as pltpu
from jax.sharding import PartitionSpec as P

BF16, F32 = jnp.bfloat16, jnp.float32
SPAN = 16
ALONG = 8
ROWS = 4
MOST = 3
EXPERTS = 8
EXTRA = 128
WIDE = ALONG * ROWS
TIGHT = ALONG * MOST
MIB = 1024 * 1024
CHUNK = 1024


def crossed_groups(ep, first):
    along_y = [[y * SPAN + i for y in range(ep // SPAN)] for i in range(SPAN)]
    along_z = [
        [y * SPAN + z * 2 + c for z in range(SPAN // 2)] for y in range(ep // SPAN) for c in range(2)
    ]
    return [g for g in along_z if g[0] % 2 == first] + [g for g in along_y if g[0] % 2 != first]


def traded(block, groups):
    return lax.all_to_all(block, "ep", 0, 0, axis_index_groups=groups, tiled=True)


def index(shape, axis):
    return lax.broadcasted_iota(jnp.int32, shape, axis).astype(F32)


def split(at, count):
    whole = jnp.floor((at + 0.5) * (1.0 / count))
    return whole, at - whole * count


def announce(rows_ref, routes_ref, weights_ref, out_ref):
    half_width = rows_ref.shape[1]
    lane = lax.broadcasted_iota(jnp.int32, (ROWS, EXTRA), 1)
    dense = jnp.zeros((ROWS, EXTRA), F32)
    routes, weights = routes_ref[...], weights_ref[...]
    for k in range(routes.shape[1]):
        name = routes[:, k : k + 1]
        dense += jnp.where((lane == name) | (lane == name + EXPERTS), weights[:, k : k + 1], 0.0)
    high = dense.astype(BF16).astype(F32)
    extra = jnp.where(lane < EXPERTS, high, dense - high)
    side = out_ref.shape[2]
    rows = rows_ref[...].astype(F32)
    rest = jnp.zeros((ROWS, 2 * side - half_width - EXTRA), F32)
    lower = jnp.concatenate([rows[:, side:], extra, rest], axis=1)
    block = jnp.concatenate([rows[:, :side], lower], axis=0).astype(BF16)
    for t in range(ALONG):
        out_ref[t] = block


def placed(half, flat):
    shape = (WIDE, 2 * WIDE) if flat else (2 * WIDE, WIDE)
    one, two = index(shape, 0 if flat else 1), index(shape, 1 if flat else 0)
    block, row = split(one, ROWS)
    return jnp.where(two == block * 2 * ROWS + half * ROWS + row, 1.0, 0.0).astype(BF16)


def sort_rows(rows_ref, out_ref, back_ref, staged, sems):
    place = lax.axis_index("ep")
    crossing, which = place % 2 == 1, (place // SPAN).astype(F32)
    full, side = out_ref.shape[1], rows_ref.shape[1]
    total = ALONG * TIGHT
    tail = rows_ref[:, full - EXTRA - side : full - side]
    tail = jnp.dot(placed(1, True), tail, preferred_element_type=F32)
    named = jnp.where((tail > 0.0) & (index((WIDE, EXTRA), 1) < EXPERTS - 0.5), 1.0, 0.0)
    one, two = index((WIDE, WIDE), 0), index((WIDE, WIDE), 1)
    ahead = jnp.where((split(one, ROWS)[0] == split(two, ROWS)[0]) & (two < one), 1.0, 0.0)
    rank = jnp.dot(ahead.astype(BF16), named.astype(BF16), preferred_element_type=F32)
    code = jnp.where(named > 0.5, rank, -1.0).astype(BF16)

    def matrix(found, at, to):
        source, slot = split(split(at, TIGHT)[1], MOST)
        block = split(to, ROWS)[0]
        return jnp.where((block == source) & (found == slot), 1.0, 0.0).astype(BF16)

    def pick(at, to):
        target = jnp.where(crossing, split(at, TIGHT)[0], which)
        return jnp.where(to == target, 1.0, 0.0).astype(BF16)

    chosen = pick(index((total, 1), 0), index((total, EXTRA), 1))
    found = lax.dot_general(chosen, code, (((1,), (1,)), ((), ())), preferred_element_type=F32)
    forth = matrix(found, index((total, 1), 0), index((1, WIDE), 1))
    copies = []
    for half, (start, end) in enumerate(((0, side), (side, full))):
        mine = jnp.dot(forth, placed(half, True), preferred_element_type=F32).astype(BF16)
        for lo in range(start, end, CHUNK):
            size = min(CHUNK, end - lo)
            at, piece = pl.ds(lo, size), rows_ref[:, pl.ds(lo - start, size)]
            staged[:, at] = jnp.dot(mine, piece, preferred_element_type=F32).astype(BF16)
            k = len(copies)
            copies.append(pltpu.make_async_copy(staged.at[:, at], out_ref.at[:, at], sems.at[k]))
            copies[k].start()
    chosen = pick(index((1, total), 1), index((EXTRA, total), 0))
    found = jnp.dot(code, chosen, preferred_element_type=F32)
    back_ref[...] = matrix(found, index((1, total), 1), index((WIDE, 1), 0))
    for copy in copies:
        copy.wait()


def gate(
    rows_ref, gain_ref, own_ref, other_hbm, kept_ref, sent_ref, squares_ref, scaled_ref, other_ref, sem
):
    copy = pltpu.make_async_copy(other_hbm, other_ref, sem)
    copy.start()
    half_width, cols = own_ref.shape[0], kept_ref.shape[1]
    rows = rows_ref.shape[0]
    deep = half_width // 7
    for k in range(7):
        at = slice(k * deep, (k + 1) * deep)
        values = rows_ref[:, at].astype(F32)
        part = jnp.sum(values * values, axis=1, keepdims=True)
        squares_ref[...] = jnp.broadcast_to(part, squares_ref.shape) + (
            squares_ref[...] if k else 0.0
        )
        scaled = (values * gain_ref[:, at].astype(F32)).astype(BF16)
        scaled_ref[:, at] = scaled
        sums = jnp.dot(scaled, own_ref[at, :], preferred_element_type=F32)
        kept_ref[:, : cols // 2] = sums + (kept_ref[:, : cols // 2] if k else 0.0)
    copy.wait()
    kept_ref[:, cols // 2 :] = jnp.dot(scaled_ref[...], other_ref[...], preferred_element_type=F32)
    sent_ref[:rows] = kept_ref[...].astype(BF16)
    across = lax.broadcasted_iota(jnp.int32, (rows, cols), 1)
    down = lax.broadcasted_iota(jnp.int32, (rows, cols), 0)
    total = jnp.sum(jnp.where(across == down, squares_ref[:, :1], 0.0), axis=0, keepdims=True)
    high = total.astype(BF16).astype(F32)
    row = lax.broadcasted_iota(jnp.int32, (16, cols), 0)
    sent_ref[rows:] = jnp.where(row == 0, high, jnp.where(row == 1, total - high, 0.0)).astype(BF16)


def expert(width, rows_ref, kept_ref, squares_ref, got_ref, down_ref, out_ref):
    units, half_width = down_ref.shape[0] // 2, down_ref.shape[1]
    which = lax.axis_index("ep") // SPAN
    tail = rows_ref[:, half_width:].astype(F32)
    lane = lax.broadcasted_iota(jnp.int32, tail.shape, 1)
    mine = (lane == which) | (lane == which + EXPERTS)
    weight = jnp.sum(jnp.where(mine, tail, 0.0), axis=1, keepdims=True)
    rows = kept_ref.shape[0]
    far = jnp.sum(got_ref[rows:].astype(F32), axis=0, keepdims=True)
    across = lax.broadcasted_iota(jnp.int32, (rows, far.shape[1]), 1)
    same = across == lax.broadcasted_iota(jnp.int32, (rows, far.shape[1]), 0)
    squares = squares_ref[:, :1] + jnp.sum(jnp.where(same, far, 0.0), axis=1, keepdims=True)
    scale = lax.rsqrt(squares * (1.0 / width) + 1e-06)
    hidden = []
    for at in range(2):
        lo = 2 * units * at
        a = (kept_ref[:, lo : lo + units] + got_ref[:rows, lo : lo + units].astype(F32)) * scale
        lo += units
        b = (kept_ref[:, lo : lo + units] + got_ref[:rows, lo : lo + units].astype(F32)) * scale
        hidden.append((a / (1.0 + jnp.exp(-a)) * b * weight).astype(BF16))
    both = jnp.concatenate(hidden, axis=1)
    deep = half_width // 4
    for k in range(4):
        at = slice(k * deep, (k + 1) * deep)
        out_ref[:, at] = jnp.dot(both, down_ref[:, at], preferred_element_type=F32).astype(BF16)


def gather_parts(back_ref, parts_ref, out_ref):
    side = out_ref.shape[1]
    for half in range(2):
        at = slice(half * side, (half + 1) * side)
        sums = jnp.dot(back_ref[...], parts_ref[:, at], preferred_element_type=F32).astype(BF16)
        part = jnp.dot(placed(half, False), sums, preferred_element_type=F32)
        both = part if half == 0 else both + part
    out_ref[...] = both.astype(BF16)


def finish(parts_ref, rows_ref, out_ref, sent_ref):
    half_width = rows_ref.shape[1]
    mixture = parts_ref[0].astype(F32)
    for t in range(1, ALONG):
        mixture += parts_ref[t].astype(F32)
    mixture = jnp.concatenate([mixture[:ROWS], mixture[ROWS:]], axis=1)
    layer = (rows_ref[...].astype(F32) + mixture).astype(BF16)
    out_ref[...] = layer
    values = layer.astype(F32)
    total = jnp.sum(values * values, axis=1, keepdims=True)
    high = total.astype(BF16).astype(F32)
    lane = lax.broadcasted_iota(jnp.int32, (ROWS, EXTRA), 1)
    pieces = jnp.where(lane == 0, high, jnp.where(lane == 1, total - high, 0.0)).astype(BF16)
    for to in range(sent_ref.shape[0]):
        sent_ref[to, :, :half_width] = layer
        sent_ref[to, :, half_width:] = pieces


def close(width, got_ref, gain_ref, out_ref):
    half_width = gain_ref.shape[1]
    crossed, side = 1 - lax.axis_index("section"), lax.axis_index("tp")
    values = got_ref[crossed * 2 + side, :, :half_width].astype(F32)
    far = got_ref[crossed * 2 + 1 - side, :, half_width:].astype(F32)
    total = jnp.sum(values * values, axis=1, keepdims=True) + jnp.sum(far, axis=1, keepdims=True)
    scale = lax.rsqrt(total * (1.0 / width) + 1e-06)
    out_ref[...] = (values * scale * gain_ref[...].astype(F32)).astype(BF16)


def local(kernel, outs, *args, spaces=None, out_spaces=None, scratch=(), vmem=24 * MIB):
    spaces = spaces or [pltpu.VMEM] * len(args)
    out_spaces = out_spaces or [pltpu.VMEM] * len(outs)
    return pl.pallas_call(
        kernel,
        out_shape=outs,
        in_specs=[pl.BlockSpec(memory_space=space) for space in spaces],
        out_specs=[pl.BlockSpec(memory_space=space) for space in out_spaces],
        scratch_shapes=list(scratch),
        compiler_params=pltpu.CompilerParams(vmem_limit_bytes=vmem),
    )(*args)


def shape(*dims, dtype=BF16):
    return jax.ShapeDtypeStruct(dims, dtype)


def body(section_rows, routes, route_weights, in_gain, gate_up, down, out_gain):
    rows = section_rows[0]
    half_width = rows.shape[1]
    ep = lax.axis_size("ep")
    width = half_width * lax.axis_size("tp")
    units = down.shape[2]
    cols = gate_up.shape[3]
    near, far = crossed_groups(ep, 1), crossed_groups(ep, 0)
    other_core = [(i, i ^ 1) for i in range(ep)]
    swap = [(0, 1), (1, 0)]
    full = half_width + EXTRA
    total = ALONG * TIGHT
    side = -(-full // (2 * EXTRA)) * EXTRA

    gate_own, down_own = gate_up[0, 0], down[0, 0]
    gate_other = lax.ppermute(gate_own, "ep", other_core)
    down_other = lax.ppermute(down_own, "ep", other_core)
    gain_other = lax.ppermute(out_gain, "section", swap)

    down_all = jnp.concatenate([down_own, down_other], axis=0)

    (leaving,) = local(
        announce,
        [shape(ALONG, 2 * ROWS, side)],
        rows,
        routes[0],
        route_weights[0],
        vmem=60 * MIB,
    )
    met = traded(leaving, near).reshape(2 * WIDE, side)
    sorted_rows, far_back = local(
        sort_rows,
        [shape(total, full), shape(WIDE, total)],
        met,
        out_spaces=[pltpu.HBM, pltpu.VMEM],
        scratch=[pltpu.VMEM((total, full), BF16), pltpu.SemaphoreType.DMA((2 * -(-side // CHUNK),))],
        vmem=53 * MIB,
    )
    gathered = traded(sorted_rows.reshape(ALONG, TIGHT, full), far).reshape(total, full)
    gathered, gain_other = lax.optimization_barrier((gathered, gain_other))
    kept, sent, squares = local(
        gate,
        [
            shape(total, 2 * cols, dtype=F32),
            shape(total + 16, 2 * cols),
            shape(total, EXTRA, dtype=F32),
        ],
        gathered,
        in_gain,
        gate_own,
        gate_other,
        spaces=[pltpu.VMEM] * 3 + [pl.ANY],
        scratch=[
            pltpu.VMEM((total, half_width), BF16),
            pltpu.VMEM((half_width, cols), BF16),
            pltpu.SemaphoreType.DMA,
        ],
    )
    got = lax.ppermute(sent, "tp", swap)
    (parts,) = local(
        functools.partial(expert, width),
        [shape(total, half_width)],
        gathered,
        kept,
        squares,
        got,
        down_all,
    )
    returned = traded(parts.reshape(ALONG, TIGHT, half_width), far).reshape(total, half_width)
    (summed,) = local(gather_parts, [shape(2 * WIDE, half_width // 2)], far_back, returned)
    home = traded(summed.reshape(ALONG, 2 * ROWS, half_width // 2), near)
    layer_out, leaving = local(
        finish, [shape(ROWS, half_width), shape(4, ROWS, full)], home, rows
    )
    got = lax.all_to_all(leaving, ("section", "tp"), 0, 0, tiled=True)
    (handed,) = local(
        functools.partial(close, width),
        [shape(ROWS, half_width)],
        got,
        gain_other,
    )
    return (layer_out[None], handed[None])


def solution(mesh):
    return jax.shard_map(
        body,
        mesh=mesh,
        in_specs=(
            P("section", "ep", "tp"),
            P("section", "ep", None),
            P("section", "ep", None),
            P("section", "tp"),
            P("section", "ep", "tp", None),
            P("section", "ep", None, "tp"),
            P("section", "tp"),
        ),
        out_specs=(P("section", "ep", "tp"), P("section", "ep", "tp")),
        check_vma=False,
    )
```

```python
import functools

import jax
import jax.numpy as jnp
from jax import lax
from jax.experimental import pallas as pl
from jax.experimental.pallas import tpu as pltpu
from jax.sharding import PartitionSpec as P

BF16, F32 = jnp.bfloat16, jnp.float32
SPAN = 16
ALONG = 8
ROWS = 4
MOST = 3
EXPERTS = 8
EXTRA = 128
WIDE = ALONG * ROWS
TIGHT = ALONG * MOST
MIB = 1024 * 1024
CHUNK = 1024


def crossed_groups(ep, first):
    along_y = [[y * SPAN + i for y in range(ep // SPAN)] for i in range(SPAN)]
    along_z = [
        [y * SPAN + z * 2 + c for z in range(SPAN // 2)] for y in range(ep // SPAN) for c in range(2)
    ]
    return [g for g in along_z if g[0] % 2 == first] + [g for g in along_y if g[0] % 2 != first]


def traded(block, groups):
    return lax.all_to_all(block, "ep", 0, 0, axis_index_groups=groups, tiled=True)


def index(shape, axis):
    return lax.broadcasted_iota(jnp.int32, shape, axis).astype(F32)


def split(at, count):
    whole = jnp.floor((at + 0.5) * (1.0 / count))
    return whole, at - whole * count


def announce(rows_ref, routes_ref, weights_ref, out_ref):
    half_width = rows_ref.shape[1]
    lane = lax.broadcasted_iota(jnp.int32, (ROWS, EXTRA), 1)
    dense = jnp.zeros((ROWS, EXTRA), F32)
    routes, weights = routes_ref[...], weights_ref[...]
    for k in range(routes.shape[1]):
        name = routes[:, k : k + 1]
        dense += jnp.where((lane == name) | (lane == name + EXPERTS), weights[:, k : k + 1], 0.0)
    high = dense.astype(BF16).astype(F32)
    extra = jnp.where(lane < EXPERTS, high, dense - high).astype(BF16)
    rows = rows_ref[...]
    for t in range(ALONG):
        out_ref[t, :, :half_width] = rows
        out_ref[t, :, half_width:] = extra


def sort_rows(rows_ref, out_ref, back_ref, staged, sems):
    place = lax.axis_index("ep")
    crossing, which = place % 2 == 1, (place // SPAN).astype(F32)
    half_width = rows_ref.shape[1] - EXTRA
    total = ALONG * TIGHT
    tail = rows_ref[:, half_width:].astype(F32)
    named = jnp.where((tail > 0.0) & (index((WIDE, EXTRA), 1) < EXPERTS - 0.5), 1.0, 0.0)
    one, two = index((WIDE, WIDE), 0), index((WIDE, WIDE), 1)
    ahead = jnp.where((split(one, ROWS)[0] == split(two, ROWS)[0]) & (two < one), 1.0, 0.0)
    rank = jnp.dot(ahead.astype(BF16), named.astype(BF16), preferred_element_type=F32)
    code = jnp.where(named > 0.5, rank, -1.0).astype(BF16)

    def matrix(found, at, to):
        source, slot = split(split(at, TIGHT)[1], MOST)
        block = split(to, ROWS)[0]
        return jnp.where((block == source) & (found == slot), 1.0, 0.0).astype(BF16)

    def pick(at, to):
        target = jnp.where(crossing, split(at, TIGHT)[0], which)
        return jnp.where(to == target, 1.0, 0.0).astype(BF16)

    chosen = pick(index((total, 1), 0), index((total, EXTRA), 1))
    found = lax.dot_general(chosen, code, (((1,), (1,)), ((), ())), preferred_element_type=F32)
    forth = matrix(found, index((total, 1), 0), index((1, WIDE), 1))
    copies = []
    for k, lo in enumerate(range(0, half_width, CHUNK)):
        at = pl.ds(lo, min(CHUNK, half_width - lo))
        staged[:, at] = jnp.dot(forth, rows_ref[:, at], preferred_element_type=F32).astype(BF16)
        copies.append(pltpu.make_async_copy(staged.at[:, at], out_ref.at[:, at], sems.at[k]))
        copies[k].start()
    chosen = pick(index((1, total), 1), index((EXTRA, total), 0))
    found = jnp.dot(code, chosen, preferred_element_type=F32)
    here = matrix(found, index((1, total), 1), index((WIDE, 1), 0)).astype(F32)
    exact = rows_ref[:, half_width:]
    high = jnp.dot(exact, chosen, preferred_element_type=F32)
    chosen = pick(index((1, total), 1), index((EXTRA, total), 0) - EXPERTS)
    low = jnp.dot(exact, chosen, preferred_element_type=F32)
    back_ref[:WIDE] = (here * high).astype(BF16)
    back_ref[WIDE:] = (here * low).astype(BF16)
    for copy in copies:
        copy.wait()


def gate(
    rows_ref, gain_ref, own_ref, other_hbm, kept_ref, sent_ref, squares_ref, scaled_ref, other_ref, sem
):
    copy = pltpu.make_async_copy(other_hbm, other_ref, sem)
    copy.start()
    half_width, cols = own_ref.shape[0], kept_ref.shape[1]
    rows = rows_ref.shape[0]
    deep = half_width // 7
    for k in range(7):
        at = slice(k * deep, (k + 1) * deep)
        values = rows_ref[:, at].astype(F32)
        part = jnp.sum(values * values, axis=1, keepdims=True)
        squares_ref[...] = jnp.broadcast_to(part, squares_ref.shape) + (
            squares_ref[...] if k else 0.0
        )
        scaled = (values * gain_ref[:, at].astype(F32)).astype(BF16)
        scaled_ref[:, at] = scaled
        sums = jnp.dot(scaled, own_ref[at, :], preferred_element_type=F32)
        kept_ref[:, : cols // 2] = sums + (kept_ref[:, : cols // 2] if k else 0.0)
    copy.wait()
    kept_ref[:, cols // 2 :] = jnp.dot(scaled_ref[...], other_ref[...], preferred_element_type=F32)
    sent_ref[:rows] = kept_ref[...].astype(BF16)
    across = lax.broadcasted_iota(jnp.int32, (rows, cols), 1)
    down = lax.broadcasted_iota(jnp.int32, (rows, cols), 0)
    total = jnp.sum(jnp.where(across == down, squares_ref[:, :1], 0.0), axis=0, keepdims=True)
    high = total.astype(BF16).astype(F32)
    row = lax.broadcasted_iota(jnp.int32, (16, cols), 0)
    sent_ref[rows:] = jnp.where(row == 0, high, jnp.where(row == 1, total - high, 0.0)).astype(BF16)


def expert(width, kept_ref, squares_ref, got_ref, down_ref, out_ref):
    units, half_width = down_ref.shape[0] // 2, down_ref.shape[1]
    rows = kept_ref.shape[0]
    far = jnp.sum(got_ref[rows:].astype(F32), axis=0, keepdims=True)
    across = lax.broadcasted_iota(jnp.int32, (rows, far.shape[1]), 1)
    same = across == lax.broadcasted_iota(jnp.int32, (rows, far.shape[1]), 0)
    squares = squares_ref[:, :1] + jnp.sum(jnp.where(same, far, 0.0), axis=1, keepdims=True)
    scale = lax.rsqrt(squares * (1.0 / width) + 1e-06)
    hidden = []
    for at in range(2):
        lo = 2 * units * at
        a = (kept_ref[:, lo : lo + units] + got_ref[:rows, lo : lo + units].astype(F32)) * scale
        lo += units
        b = (kept_ref[:, lo : lo + units] + got_ref[:rows, lo : lo + units].astype(F32)) * scale
        hidden.append((a / (1.0 + jnp.exp(-a)) * b).astype(BF16))
    both = jnp.concatenate(hidden, axis=1)
    deep = half_width // 4
    for k in range(4):
        at = slice(k * deep, (k + 1) * deep)
        out_ref[:, at] = jnp.dot(both, down_ref[:, at], preferred_element_type=F32).astype(BF16)


def gather_parts(back_ref, parts_ref, out_ref):
    sums = jnp.dot(back_ref[...], parts_ref[...], preferred_element_type=F32)
    out_ref[...] = (sums[:WIDE] + sums[WIDE:]).astype(BF16)


def finish(parts_ref, rows_ref, out_ref, sent_ref):
    half_width = rows_ref.shape[1]
    mixture = parts_ref[0].astype(F32)
    for t in range(1, ALONG):
        mixture += parts_ref[t].astype(F32)
    layer = (rows_ref[...].astype(F32) + mixture).astype(BF16)
    out_ref[...] = layer
    values = layer.astype(F32)
    total = jnp.sum(values * values, axis=1, keepdims=True)
    high = total.astype(BF16).astype(F32)
    lane = lax.broadcasted_iota(jnp.int32, (ROWS, EXTRA), 1)
    pieces = jnp.where(lane == 0, high, jnp.where(lane == 1, total - high, 0.0)).astype(BF16)
    for to in range(sent_ref.shape[0]):
        sent_ref[to, :, :half_width] = layer
        sent_ref[to, :, half_width:] = pieces


def close(width, got_ref, gain_ref, out_ref):
    half_width = gain_ref.shape[1]
    crossed, side = 1 - lax.axis_index("section"), lax.axis_index("tp")
    values = got_ref[crossed * 2 + side, :, :half_width].astype(F32)
    far = got_ref[crossed * 2 + 1 - side, :, half_width:].astype(F32)
    total = jnp.sum(values * values, axis=1, keepdims=True) + jnp.sum(far, axis=1, keepdims=True)
    scale = lax.rsqrt(total * (1.0 / width) + 1e-06)
    out_ref[...] = (values * scale * gain_ref[...].astype(F32)).astype(BF16)


def local(kernel, outs, *args, spaces=None, out_spaces=None, scratch=(), vmem=24 * MIB):
    spaces = spaces or [pltpu.VMEM] * len(args)
    out_spaces = out_spaces or [pltpu.VMEM] * len(outs)
    return pl.pallas_call(
        kernel,
        out_shape=outs,
        in_specs=[pl.BlockSpec(memory_space=space) for space in spaces],
        out_specs=[pl.BlockSpec(memory_space=space) for space in out_spaces],
        scratch_shapes=list(scratch),
        compiler_params=pltpu.CompilerParams(vmem_limit_bytes=vmem),
    )(*args)


def shape(*dims, dtype=BF16):
    return jax.ShapeDtypeStruct(dims, dtype)


def body(section_rows, routes, route_weights, in_gain, gate_up, down, out_gain):
    rows = section_rows[0]
    half_width = rows.shape[1]
    ep = lax.axis_size("ep")
    width = half_width * lax.axis_size("tp")
    units = down.shape[2]
    cols = gate_up.shape[3]
    near, far = crossed_groups(ep, 1), crossed_groups(ep, 0)
    other_core = [(i, i ^ 1) for i in range(ep)]
    swap = [(0, 1), (1, 0)]
    full = half_width + EXTRA
    total = ALONG * TIGHT

    gate_own, down_own = gate_up[0, 0], down[0, 0]
    gate_other = lax.ppermute(gate_own, "ep", other_core)
    down_other = lax.ppermute(down_own, "ep", other_core)
    gain_other = lax.ppermute(out_gain, "section", swap)

    down_all = jnp.concatenate([down_own, down_other], axis=0)

    (leaving,) = local(
        announce,
        [shape(ALONG, ROWS, full)],
        rows,
        routes[0],
        route_weights[0],
        vmem=60 * MIB,
    )
    met = traded(leaving, near).reshape(WIDE, full)
    sorted_rows, far_back = local(
        sort_rows,
        [shape(total, half_width), shape(2 * WIDE, total)],
        met,
        out_spaces=[pltpu.HBM, pltpu.VMEM],
        scratch=[
            pltpu.VMEM((total, half_width), BF16),
            pltpu.SemaphoreType.DMA((-(-half_width // CHUNK),)),
        ],
        vmem=53 * MIB,
    )
    gathered = traded(sorted_rows.reshape(ALONG, TIGHT, half_width), far)
    gathered = gathered.reshape(total, half_width)
    gathered, gain_other = lax.optimization_barrier((gathered, gain_other))
    kept, sent, squares = local(
        gate,
        [
            shape(total, 2 * cols, dtype=F32),
            shape(total + 16, 2 * cols),
            shape(total, EXTRA, dtype=F32),
        ],
        gathered,
        in_gain,
        gate_own,
        gate_other,
        spaces=[pltpu.VMEM] * 3 + [pl.ANY],
        scratch=[
            pltpu.VMEM((total, half_width), BF16),
            pltpu.VMEM((half_width, cols), BF16),
            pltpu.SemaphoreType.DMA,
        ],
    )
    got = lax.ppermute(sent, "tp", swap)
    (parts,) = local(
        functools.partial(expert, width),
        [shape(total, half_width)],
        kept,
        squares,
        got,
        down_all,
    )
    returned = traded(parts.reshape(ALONG, TIGHT, half_width), far).reshape(total, half_width)
    (summed,) = local(gather_parts, [shape(WIDE, half_width)], far_back, returned)
    home = traded(summed.reshape(ALONG, ROWS, half_width), near)
    layer_out, leaving = local(
        finish, [shape(ROWS, half_width), shape(4, ROWS, full)], home, rows
    )
    got = lax.all_to_all(leaving, ("section", "tp"), 0, 0, tiled=True)
    (handed,) = local(
        functools.partial(close, width),
        [shape(ROWS, half_width)],
        got,
        gain_other,
    )
    return (layer_out[None], handed[None])


def solution(mesh):
    return jax.shard_map(
        body,
        mesh=mesh,
        in_specs=(
            P("section", "ep", "tp"),
            P("section", "ep", None),
            P("section", "ep", None),
            P("section", "tp"),
            P("section", "ep", "tp", None),
            P("section", "ep", None, "tp"),
            P("section", "tp"),
        ),
        out_specs=(P("section", "ep", "tp"), P("section", "ep", "tp")),
        check_vma=False,
    )
```

```python
import functools

import jax
import jax.numpy as jnp
from jax import lax
from jax.experimental import pallas as pl
from jax.experimental.pallas import tpu as pltpu
from jax.sharding import PartitionSpec as P

BF16, F32 = jnp.bfloat16, jnp.float32
SPAN = 16
ALONG = 8
ROWS = 4
MOST = 3
EXPERTS = 8
EXTRA = 128
WIDE = ALONG * ROWS
TIGHT = ALONG * MOST
MIB = 1024 * 1024
CHUNK = 1024
PIECES = 7


def crossed_groups(ep, first):
    along_y = [[y * SPAN + i for y in range(ep // SPAN)] for i in range(SPAN)]
    along_z = [
        [y * SPAN + z * 2 + c for z in range(SPAN // 2)] for y in range(ep // SPAN) for c in range(2)
    ]
    return [g for g in along_z if g[0] % 2 == first] + [g for g in along_y if g[0] % 2 != first]


def traded(block, groups):
    return lax.all_to_all(block, "ep", 0, 0, axis_index_groups=groups, tiled=True)


def index(shape, axis):
    return lax.broadcasted_iota(jnp.int32, shape, axis).astype(F32)


def split(at, count):
    whole = jnp.floor((at + 0.5) * (1.0 / count))
    return whole, at - whole * count


def announce(rows_ref, routes_ref, weights_ref, out_ref):
    half_width = rows_ref.shape[1]
    lane = lax.broadcasted_iota(jnp.int32, (ROWS, EXTRA), 1)
    dense = jnp.zeros((ROWS, EXTRA), F32)
    routes, weights = routes_ref[...], weights_ref[...]
    for k in range(routes.shape[1]):
        name = routes[:, k : k + 1]
        dense += jnp.where((lane == name) | (lane == name + EXPERTS), weights[:, k : k + 1], 0.0)
    high = dense.astype(BF16).astype(F32)
    extra = jnp.where(lane < EXPERTS, high, dense - high).astype(BF16)
    rows = rows_ref[...]
    for t in range(ALONG):
        out_ref[t, :, :half_width] = rows
        out_ref[t, :, half_width:] = extra


def sort_rows(rows_ref, out_ref, back_ref, staged, sems):
    place = lax.axis_index("ep")
    crossing, which = place % 2 == 1, (place // SPAN).astype(F32)
    half_width = rows_ref.shape[1] - EXTRA
    total = ALONG * TIGHT
    tail = rows_ref[:, half_width:].astype(F32)
    named = jnp.where((tail > 0.0) & (index((WIDE, EXTRA), 1) < EXPERTS - 0.5), 1.0, 0.0)
    one, two = index((WIDE, WIDE), 0), index((WIDE, WIDE), 1)
    ahead = jnp.where((split(one, ROWS)[0] == split(two, ROWS)[0]) & (two < one), 1.0, 0.0)
    rank = jnp.dot(ahead.astype(BF16), named.astype(BF16), preferred_element_type=F32)
    code = jnp.where(named > 0.5, rank, -1.0).astype(BF16)

    def matrix(found, at, to):
        source, slot = split(split(at, TIGHT)[1], MOST)
        block = split(to, ROWS)[0]
        return jnp.where((block == source) & (found == slot), 1.0, 0.0).astype(BF16)

    def pick(at, to):
        target = jnp.where(crossing, split(at, TIGHT)[0], which)
        return jnp.where(to == target, 1.0, 0.0).astype(BF16)

    chosen = pick(index((total, 1), 0), index((total, EXTRA), 1))
    found = lax.dot_general(chosen, code, (((1,), (1,)), ((), ())), preferred_element_type=F32)
    forth = matrix(found, index((total, 1), 0), index((1, WIDE), 1))
    copies = []
    for k, lo in enumerate(range(0, half_width, CHUNK)):
        at = pl.ds(lo, min(CHUNK, half_width - lo))
        staged[:, at] = jnp.dot(forth, rows_ref[:, at], preferred_element_type=F32).astype(BF16)
        copies.append(pltpu.make_async_copy(staged.at[:, at], out_ref.at[:, at], sems.at[k]))
        copies[k].start()
    chosen = pick(index((1, total), 1), index((EXTRA, total), 0))
    found = jnp.dot(code, chosen, preferred_element_type=F32)
    here = matrix(found, index((1, total), 1), index((WIDE, 1), 0)).astype(F32)
    exact = rows_ref[:, half_width:]
    high = jnp.dot(exact, chosen, preferred_element_type=F32)
    chosen = pick(index((1, total), 1), index((EXTRA, total), 0) - EXPERTS)
    low = jnp.dot(exact, chosen, preferred_element_type=F32)
    back_ref[:WIDE] = (here * high).astype(BF16)
    back_ref[WIDE:] = (here * low).astype(BF16)
    for copy in copies:
        copy.wait()


def gate(
    rows_ref, gain_ref, own_ref, other_hbm, kept_ref, sent_ref, squares_ref, other_ref, sems
):
    half_width, cols = own_ref.shape[0], kept_ref.shape[1]
    rows = rows_ref.shape[0]
    deep = half_width // PIECES
    copies = []
    for k in range(PIECES):
        at = pl.ds(k * deep, deep)
        copies.append(pltpu.make_async_copy(other_hbm.at[at], other_ref.at[at], sems.at[k]))
        copies[k].start()
    for k in range(PIECES):
        at = slice(k * deep, (k + 1) * deep)
        values = rows_ref[:, at].astype(F32)
        pieces = values * values
        part = pieces[:, :EXTRA]
        for lo in range(EXTRA, deep, EXTRA):
            part = part + pieces[:, lo : lo + EXTRA]
        squares_ref[...] = part + (squares_ref[...] if k else 0.0)
        scaled = (values * gain_ref[:, at].astype(F32)).astype(BF16)
        sums = jnp.dot(scaled, own_ref[at, :], preferred_element_type=F32)
        kept_ref[:, : cols // 2] = sums + (kept_ref[:, : cols // 2] if k else 0.0)
        copies[k].wait()
        sums = jnp.dot(scaled, other_ref[at, :], preferred_element_type=F32)
        kept_ref[:, cols // 2 :] = sums + (kept_ref[:, cols // 2 :] if k else 0.0)
    squares = jnp.sum(squares_ref[...], axis=1, keepdims=True)
    squares_ref[...] = jnp.broadcast_to(squares, squares_ref.shape)
    sent_ref[:rows] = kept_ref[...].astype(BF16)
    across = lax.broadcasted_iota(jnp.int32, (rows, cols), 1)
    down = lax.broadcasted_iota(jnp.int32, (rows, cols), 0)
    total = jnp.sum(jnp.where(across == down, squares, 0.0), axis=0, keepdims=True)
    high = total.astype(BF16).astype(F32)
    row = lax.broadcasted_iota(jnp.int32, (16, cols), 0)
    sent_ref[rows:] = jnp.where(row == 0, high, jnp.where(row == 1, total - high, 0.0)).astype(BF16)


def expert(width, kept_ref, squares_ref, got_ref, down_ref, out_ref):
    units, half_width = down_ref.shape[0] // 2, down_ref.shape[1]
    rows = kept_ref.shape[0]
    far = jnp.sum(got_ref[rows:].astype(F32), axis=0, keepdims=True)
    across = lax.broadcasted_iota(jnp.int32, (rows, far.shape[1]), 1)
    same = across == lax.broadcasted_iota(jnp.int32, (rows, far.shape[1]), 0)
    squares = squares_ref[:, :1] + jnp.sum(jnp.where(same, far, 0.0), axis=1, keepdims=True)
    scale = lax.rsqrt(squares * (1.0 / width) + 1e-06)
    hidden = []
    for at in range(2):
        lo = 2 * units * at
        a = (kept_ref[:, lo : lo + units] + got_ref[:rows, lo : lo + units].astype(F32)) * scale
        lo += units
        b = (kept_ref[:, lo : lo + units] + got_ref[:rows, lo : lo + units].astype(F32)) * scale
        hidden.append((a / (1.0 + jnp.exp(-a)) * b).astype(BF16))
    both = jnp.concatenate(hidden, axis=1)
    deep = half_width // 4
    for k in range(4):
        at = slice(k * deep, (k + 1) * deep)
        out_ref[:, at] = jnp.dot(both, down_ref[:, at], preferred_element_type=F32).astype(BF16)


def gather_parts(back_ref, parts_ref, out_ref):
    sums = jnp.dot(back_ref[...], parts_ref[...], preferred_element_type=F32)
    sums = (sums[:WIDE] + sums[WIDE:]).astype(BF16)
    for t in range(ALONG):
        out_ref[t] = sums[t * ROWS : (t + 1) * ROWS]


def finish(parts_ref, rows_ref, out_ref, sent_ref):
    half_width = rows_ref.shape[1]
    mixture = parts_ref[0].astype(F32)
    for t in range(1, ALONG):
        mixture += parts_ref[t].astype(F32)
    layer = (rows_ref[...].astype(F32) + mixture).astype(BF16)
    out_ref[...] = layer
    values = layer.astype(F32)
    total = jnp.sum(values * values, axis=1, keepdims=True)
    high = total.astype(BF16).astype(F32)
    lane = lax.broadcasted_iota(jnp.int32, (ROWS, EXTRA), 1)
    pieces = jnp.where(lane == 0, high, jnp.where(lane == 1, total - high, 0.0)).astype(BF16)
    for to in range(sent_ref.shape[0]):
        sent_ref[to, :, :half_width] = layer
        sent_ref[to, :, half_width:] = pieces


def close(width, got_ref, gain_ref, out_ref):
    half_width = gain_ref.shape[1]
    crossed, side = 1 - lax.axis_index("section"), lax.axis_index("tp")
    values = got_ref[crossed * 2 + side, :, :half_width].astype(F32)
    far = got_ref[crossed * 2 + 1 - side, :, half_width:].astype(F32)
    total = jnp.sum(values * values, axis=1, keepdims=True) + jnp.sum(far, axis=1, keepdims=True)
    scale = lax.rsqrt(total * (1.0 / width) + 1e-06)
    out_ref[...] = (values * scale * gain_ref[...].astype(F32)).astype(BF16)


def local(kernel, outs, *args, spaces=None, out_spaces=None, scratch=(), vmem=24 * MIB):
    spaces = spaces or [pltpu.VMEM] * len(args)
    out_spaces = out_spaces or [pltpu.VMEM] * len(outs)
    return pl.pallas_call(
        kernel,
        out_shape=outs,
        in_specs=[pl.BlockSpec(memory_space=space) for space in spaces],
        out_specs=[pl.BlockSpec(memory_space=space) for space in out_spaces],
        scratch_shapes=list(scratch),
        compiler_params=pltpu.CompilerParams(vmem_limit_bytes=vmem),
    )(*args)


def shape(*dims, dtype=BF16):
    return jax.ShapeDtypeStruct(dims, dtype)


def body(section_rows, routes, route_weights, in_gain, gate_up, down, out_gain):
    rows = section_rows[0]
    half_width = rows.shape[1]
    ep = lax.axis_size("ep")
    width = half_width * lax.axis_size("tp")
    units = down.shape[2]
    cols = gate_up.shape[3]
    near, far = crossed_groups(ep, 1), crossed_groups(ep, 0)
    other_core = [(i, i ^ 1) for i in range(ep)]
    swap = [(0, 1), (1, 0)]
    full = half_width + EXTRA
    total = ALONG * TIGHT

    gate_own, down_own = gate_up[0, 0], down[0, 0]
    gate_other = lax.ppermute(gate_own, "ep", other_core)
    down_other = lax.ppermute(down_own, "ep", other_core)
    gain_other = lax.ppermute(out_gain, "section", swap)

    down_all = jnp.concatenate([down_own, down_other], axis=0)

    (leaving,) = local(
        announce,
        [shape(ALONG, ROWS, full)],
        rows,
        routes[0],
        route_weights[0],
        vmem=60 * MIB,
    )
    met = traded(leaving, near).reshape(WIDE, full)
    sorted_rows, far_back = local(
        sort_rows,
        [shape(total, half_width), shape(2 * WIDE, total)],
        met,
        out_spaces=[pltpu.HBM, pltpu.VMEM],
        scratch=[
            pltpu.VMEM((total, half_width), BF16),
            pltpu.SemaphoreType.DMA((-(-half_width // CHUNK),)),
        ],
        vmem=53 * MIB,
    )
    gathered = traded(sorted_rows.reshape(ALONG, TIGHT, half_width), far)
    gathered = gathered.reshape(total, half_width)
    gathered, gain_other = lax.optimization_barrier((gathered, gain_other))
    kept, sent, squares = local(
        gate,
        [
            shape(total, 2 * cols, dtype=F32),
            shape(total + 16, 2 * cols),
            shape(total, EXTRA, dtype=F32),
        ],
        gathered,
        in_gain,
        gate_own,
        gate_other,
        spaces=[pltpu.VMEM] * 3 + [pl.ANY],
        scratch=[
            pltpu.VMEM((half_width, cols), BF16),
            pltpu.SemaphoreType.DMA((PIECES,)),
        ],
    )
    got = lax.ppermute(sent, "tp", swap)
    (parts,) = local(
        functools.partial(expert, width),
        [shape(total, half_width)],
        kept,
        squares,
        got,
        down_all,
    )
    returned = traded(parts.reshape(ALONG, TIGHT, half_width), far).reshape(total, half_width)
    (summed,) = local(gather_parts, [shape(ALONG, ROWS, half_width)], far_back, returned)
    home = traded(summed, near)
    layer_out, leaving = local(
        finish, [shape(ROWS, half_width), shape(4, ROWS, full)], home, rows
    )
    got = lax.all_to_all(leaving, ("section", "tp"), 0, 0, tiled=True)
    (handed,) = local(
        functools.partial(close, width),
        [shape(ROWS, half_width)],
        got,
        gain_other,
    )
    return (layer_out[None], handed[None])


def solution(mesh):
    return jax.shard_map(
        body,
        mesh=mesh,
        in_specs=(
            P("section", "ep", "tp"),
            P("section", "ep", None),
            P("section", "ep", None),
            P("section", "tp"),
            P("section", "ep", "tp", None),
            P("section", "ep", None, "tp"),
            P("section", "tp"),
        ),
        out_specs=(P("section", "ep", "tp"), P("section", "ep", "tp")),
        check_vma=False,
    )
```

```python
import functools

import jax
import jax.numpy as jnp
from jax import lax
from jax.experimental import pallas as pl
from jax.experimental.pallas import tpu as pltpu
from jax.sharding import PartitionSpec as P

BF16, F32 = jnp.bfloat16, jnp.float32
SPAN = 16
ALONG = 8
ROWS = 4
MOST = 3
EXPERTS = 8
EXTRA = 128
WIDE = ALONG * ROWS
TIGHT = ALONG * MOST
MIB = 1024 * 1024
CHUNK = 512
PIECES = 7


def crossed_groups(ep, first):
    along_y = [[y * SPAN + i for y in range(ep // SPAN)] for i in range(SPAN)]
    along_z = [
        [y * SPAN + z * 2 + c for z in range(SPAN // 2)] for y in range(ep // SPAN) for c in range(2)
    ]
    return [g for g in along_z if g[0] % 2 == first] + [g for g in along_y if g[0] % 2 != first]


def traded(block, groups):
    return lax.all_to_all(block, "ep", 0, 0, axis_index_groups=groups, tiled=True)


def index(shape, axis):
    return lax.broadcasted_iota(jnp.int32, shape, axis).astype(F32)


def split(at, count):
    whole = jnp.floor((at + 0.5) * (1.0 / count))
    return whole, at - whole * count


def announce(rows_ref, routes_ref, weights_ref, out_ref):
    half_width = rows_ref.shape[1]
    lane = lax.broadcasted_iota(jnp.int32, (ROWS, EXTRA), 1)
    dense = jnp.zeros((ROWS, EXTRA), F32)
    routes, weights = routes_ref[...], weights_ref[...]
    for k in range(routes.shape[1]):
        name = routes[:, k : k + 1]
        dense += jnp.where((lane == name) | (lane == name + EXPERTS), weights[:, k : k + 1], 0.0)
    high = dense.astype(BF16).astype(F32)
    extra = jnp.where(lane < EXPERTS, high, dense - high).astype(BF16)
    rows = rows_ref[...]
    for t in range(ALONG):
        out_ref[t, :, :half_width] = rows
        out_ref[t, :, half_width:] = extra


def sort_rows(rows_ref, out_ref, back_ref, staged, sems):
    place = lax.axis_index("ep")
    crossing, which = place % 2 == 1, (place // SPAN).astype(F32)
    half_width = rows_ref.shape[1] - EXTRA
    total = ALONG * TIGHT
    tail = rows_ref[:, half_width:].astype(F32)
    named = jnp.where((tail > 0.0) & (index((WIDE, EXTRA), 1) < EXPERTS - 0.5), 1.0, 0.0)
    one, two = index((WIDE, WIDE), 0), index((WIDE, WIDE), 1)
    ahead = jnp.where((split(one, ROWS)[0] == split(two, ROWS)[0]) & (two < one), 1.0, 0.0)
    rank = jnp.dot(ahead.astype(BF16), named.astype(BF16), preferred_element_type=F32)
    code = jnp.where(named > 0.5, rank, -1.0).astype(BF16)

    def matrix(found, at, to):
        source, slot = split(split(at, TIGHT)[1], MOST)
        block = split(to, ROWS)[0]
        return jnp.where((block == source) & (found == slot), 1.0, 0.0).astype(BF16)

    def pick(at, to):
        target = jnp.where(crossing, split(at, TIGHT)[0], which)
        return jnp.where(to == target, 1.0, 0.0).astype(BF16)

    chosen = pick(index((total, 1), 0), index((total, EXTRA), 1))
    found = lax.dot_general(chosen, code, (((1,), (1,)), ((), ())), preferred_element_type=F32)
    forth = matrix(found, index((total, 1), 0), index((1, WIDE), 1))
    copies = []
    for k, lo in enumerate(range(0, half_width, CHUNK)):
        at = pl.ds(lo, min(CHUNK, half_width - lo))
        staged[:, at] = jnp.dot(forth, rows_ref[:, at], preferred_element_type=F32).astype(BF16)
        copies.append(pltpu.make_async_copy(staged.at[:, at], out_ref.at[:, at], sems.at[k]))
        copies[k].start()
    chosen = pick(index((1, total), 1), index((EXTRA, total), 0))
    found = jnp.dot(code, chosen, preferred_element_type=F32)
    here = matrix(found, index((1, total), 1), index((WIDE, 1), 0)).astype(F32)
    exact = rows_ref[:, half_width:]
    high = jnp.dot(exact, chosen, preferred_element_type=F32)
    chosen = pick(index((1, total), 1), index((EXTRA, total), 0) - EXPERTS)
    low = jnp.dot(exact, chosen, preferred_element_type=F32)
    back_ref[:WIDE] = (here * high).astype(BF16)
    back_ref[WIDE:] = (here * low).astype(BF16)
    for copy in copies:
        copy.wait()


def gate(
    rows_ref, gain_ref, own_ref, other_hbm, kept_ref, sent_ref, squares_ref, other_ref, sems
):
    half_width, cols = own_ref.shape[0], kept_ref.shape[1]
    rows = rows_ref.shape[0]
    deep = half_width // PIECES
    copies = []
    for k in range(PIECES):
        at = pl.ds(k * deep, deep)
        copies.append(pltpu.make_async_copy(other_hbm.at[at], other_ref.at[at], sems.at[k]))
        copies[k].start()
    for k in range(PIECES):
        at = slice(k * deep, (k + 1) * deep)
        values = rows_ref[:, at].astype(F32)
        pieces = values * values
        part = pieces[:, :EXTRA]
        for lo in range(EXTRA, deep, EXTRA):
            part = part + pieces[:, lo : lo + EXTRA]
        squares_ref[...] = part + (squares_ref[...] if k else 0.0)
        scaled = (values * gain_ref[:, at].astype(F32)).astype(BF16)
        sums = jnp.dot(scaled, own_ref[at, :], preferred_element_type=F32)
        kept_ref[:, : cols // 2] = sums + (kept_ref[:, : cols // 2] if k else 0.0)
        copies[k].wait()
        sums = jnp.dot(scaled, other_ref[at, :], preferred_element_type=F32)
        kept_ref[:, cols // 2 :] = sums + (kept_ref[:, cols // 2 :] if k else 0.0)
    squares = jnp.sum(squares_ref[...], axis=1, keepdims=True)
    squares_ref[...] = jnp.broadcast_to(squares, squares_ref.shape)
    sent_ref[:rows] = kept_ref[...].astype(BF16)
    across = lax.broadcasted_iota(jnp.int32, (rows, cols), 1)
    down = lax.broadcasted_iota(jnp.int32, (rows, cols), 0)
    total = jnp.sum(jnp.where(across == down, squares, 0.0), axis=0, keepdims=True)
    high = total.astype(BF16).astype(F32)
    row = lax.broadcasted_iota(jnp.int32, (16, cols), 0)
    sent_ref[rows:] = jnp.where(row == 0, high, jnp.where(row == 1, total - high, 0.0)).astype(BF16)


def expert(width, kept_ref, squares_ref, got_ref, down_ref, out_ref):
    units, half_width = down_ref.shape[0] // 2, down_ref.shape[1]
    rows = kept_ref.shape[0]
    far = jnp.sum(got_ref[rows:].astype(F32), axis=0, keepdims=True)
    across = lax.broadcasted_iota(jnp.int32, (rows, far.shape[1]), 1)
    same = across == lax.broadcasted_iota(jnp.int32, (rows, far.shape[1]), 0)
    squares = squares_ref[:, :1] + jnp.sum(jnp.where(same, far, 0.0), axis=1, keepdims=True)
    scale = lax.rsqrt(squares * (1.0 / width) + 1e-06)
    hidden = []
    for at in range(2):
        lo = 2 * units * at
        a = (kept_ref[:, lo : lo + units] + got_ref[:rows, lo : lo + units].astype(F32)) * scale
        lo += units
        b = (kept_ref[:, lo : lo + units] + got_ref[:rows, lo : lo + units].astype(F32)) * scale
        hidden.append((a / (1.0 + jnp.exp(-a)) * b).astype(BF16))
    both = jnp.concatenate(hidden, axis=1)
    deep = half_width // 4
    for k in range(4):
        at = slice(k * deep, (k + 1) * deep)
        out_ref[:, at] = jnp.dot(both, down_ref[:, at], preferred_element_type=F32).astype(BF16)


def gather_parts(back_ref, parts_ref, out_ref):
    sums = jnp.dot(back_ref[...], parts_ref[...], preferred_element_type=F32)
    sums = (sums[:WIDE] + sums[WIDE:]).astype(BF16)
    for t in range(ALONG):
        out_ref[t] = sums[t * ROWS : (t + 1) * ROWS]


def finish(parts_ref, rows_ref, out_ref, sent_ref):
    half_width = rows_ref.shape[1]
    mixture = parts_ref[0].astype(F32)
    for t in range(1, ALONG):
        mixture += parts_ref[t].astype(F32)
    layer = (rows_ref[...].astype(F32) + mixture).astype(BF16)
    out_ref[...] = layer
    values = layer.astype(F32)
    total = jnp.sum(values * values, axis=1, keepdims=True)
    high = total.astype(BF16).astype(F32)
    lane = lax.broadcasted_iota(jnp.int32, (ROWS, EXTRA), 1)
    pieces = jnp.where(lane == 0, high, jnp.where(lane == 1, total - high, 0.0)).astype(BF16)
    for to in range(sent_ref.shape[0]):
        sent_ref[to, :, :half_width] = layer
        sent_ref[to, :, half_width:] = pieces


def close(width, got_ref, gain_ref, out_ref):
    half_width = gain_ref.shape[1]
    crossed, side = 1 - lax.axis_index("section"), lax.axis_index("tp")
    values = got_ref[crossed * 2 + side, :, :half_width].astype(F32)
    far = got_ref[crossed * 2 + 1 - side, :, half_width:].astype(F32)
    total = jnp.sum(values * values, axis=1, keepdims=True) + jnp.sum(far, axis=1, keepdims=True)
    scale = lax.rsqrt(total * (1.0 / width) + 1e-06)
    out_ref[...] = (values * scale * gain_ref[...].astype(F32)).astype(BF16)


def local(kernel, outs, *args, spaces=None, out_spaces=None, scratch=(), vmem=24 * MIB):
    spaces = spaces or [pltpu.VMEM] * len(args)
    out_spaces = out_spaces or [pltpu.VMEM] * len(outs)
    return pl.pallas_call(
        kernel,
        out_shape=outs,
        in_specs=[pl.BlockSpec(memory_space=space) for space in spaces],
        out_specs=[pl.BlockSpec(memory_space=space) for space in out_spaces],
        scratch_shapes=list(scratch),
        compiler_params=pltpu.CompilerParams(vmem_limit_bytes=vmem),
    )(*args)


def shape(*dims, dtype=BF16):
    return jax.ShapeDtypeStruct(dims, dtype)


def body(section_rows, routes, route_weights, in_gain, gate_up, down, out_gain):
    rows = section_rows[0]
    half_width = rows.shape[1]
    ep = lax.axis_size("ep")
    width = half_width * lax.axis_size("tp")
    units = down.shape[2]
    cols = gate_up.shape[3]
    near, far = crossed_groups(ep, 1), crossed_groups(ep, 0)
    other_core = [(i, i ^ 1) for i in range(ep)]
    swap = [(0, 1), (1, 0)]
    full = half_width + EXTRA
    total = ALONG * TIGHT

    gate_own, down_own = gate_up[0, 0], down[0, 0]
    gate_other = lax.ppermute(gate_own, "ep", other_core)
    down_other = lax.ppermute(down_own, "ep", other_core)
    gain_other = lax.ppermute(out_gain, "section", swap)

    down_all = jnp.concatenate([down_own, down_other], axis=0)

    (leaving,) = local(
        announce,
        [shape(ALONG, ROWS, full)],
        rows,
        routes[0],
        route_weights[0],
        vmem=60 * MIB,
    )
    met = traded(leaving, near).reshape(WIDE, full)
    sorted_rows, far_back = local(
        sort_rows,
        [shape(total, half_width), shape(2 * WIDE, total)],
        met,
        out_spaces=[pltpu.HBM, pltpu.VMEM],
        scratch=[
            pltpu.VMEM((total, half_width), BF16),
            pltpu.SemaphoreType.DMA((-(-half_width // CHUNK),)),
        ],
        vmem=53 * MIB,
    )
    gathered = traded(sorted_rows.reshape(ALONG, TIGHT, half_width), far)
    gathered = gathered.reshape(total, half_width)
    gathered, gain_other = lax.optimization_barrier((gathered, gain_other))
    kept, sent, squares = local(
        gate,
        [
            shape(total, 2 * cols, dtype=F32),
            shape(total + 16, 2 * cols),
            shape(total, EXTRA, dtype=F32),
        ],
        gathered,
        in_gain,
        gate_own,
        gate_other,
        spaces=[pltpu.VMEM] * 3 + [pl.ANY],
        scratch=[
            pltpu.VMEM((half_width, cols), BF16),
            pltpu.SemaphoreType.DMA((PIECES,)),
        ],
    )
    got = lax.ppermute(sent, "tp", swap)
    (parts,) = local(
        functools.partial(expert, width),
        [shape(total, half_width)],
        kept,
        squares,
        got,
        down_all,
    )
    returned = traded(parts.reshape(ALONG, TIGHT, half_width), far).reshape(total, half_width)
    (summed,) = local(gather_parts, [shape(ALONG, ROWS, half_width)], far_back, returned)
    home = traded(summed, near)
    layer_out, leaving = local(
        finish, [shape(ROWS, half_width), shape(4, ROWS, full)], home, rows
    )
    got = lax.all_to_all(leaving, ("section", "tp"), 0, 0, tiled=True)
    (handed,) = local(
        functools.partial(close, width),
        [shape(ROWS, half_width)],
        got,
        gain_other,
    )
    return (layer_out[None], handed[None])


def solution(mesh):
    return jax.shard_map(
        body,
        mesh=mesh,
        in_specs=(
            P("section", "ep", "tp"),
            P("section", "ep", None),
            P("section", "ep", None),
            P("section", "tp"),
            P("section", "ep", "tp", None),
            P("section", "ep", None, "tp"),
            P("section", "tp"),
        ),
        out_specs=(P("section", "ep", "tp"), P("section", "ep", "tp")),
        check_vma=False,
    )
```

```python
import functools

import jax
import jax.numpy as jnp
from jax import lax
from jax.experimental import pallas as pl
from jax.experimental.pallas import tpu as pltpu
from jax.sharding import PartitionSpec as P

BF16, F32 = jnp.bfloat16, jnp.float32
SPAN = 16
ALONG = 8
ROWS = 4
MOST = 3
EXPERTS = 8
EXTRA = 128
WIDE = ALONG * ROWS
TIGHT = ALONG * MOST
MIB = 1024 * 1024
CHUNK = 1024
PIECES = 7


def crossed_groups(ep, first):
    along_y = [[y * SPAN + i for y in range(ep // SPAN)] for i in range(SPAN)]
    along_z = [
        [y * SPAN + z * 2 + c for z in range(SPAN // 2)] for y in range(ep // SPAN) for c in range(2)
    ]
    return [g for g in along_z if g[0] % 2 == first] + [g for g in along_y if g[0] % 2 != first]


def traded(block, groups):
    return lax.all_to_all(block, "ep", 0, 0, axis_index_groups=groups, tiled=True)


def index(shape, axis):
    return lax.broadcasted_iota(jnp.int32, shape, axis).astype(F32)


def split(at, count):
    whole = jnp.floor((at + 0.5) * (1.0 / count))
    return whole, at - whole * count


def announce(rows_ref, routes_ref, weights_ref, out_ref):
    half_width = rows_ref.shape[1]
    lane = lax.broadcasted_iota(jnp.int32, (ROWS, EXTRA), 1)
    dense = jnp.zeros((ROWS, EXTRA), F32)
    routes, weights = routes_ref[...], weights_ref[...]
    for k in range(routes.shape[1]):
        name = routes[:, k : k + 1]
        dense += jnp.where((lane == name) | (lane == name + EXPERTS), weights[:, k : k + 1], 0.0)
    high = dense.astype(BF16).astype(F32)
    extra = jnp.where(lane < EXPERTS, high, dense - high).astype(BF16)
    rows = rows_ref[...]
    for t in range(ALONG):
        out_ref[t, :, :half_width] = rows
        out_ref[t, :, half_width:] = extra


def sort_rows(rows_ref, out_ref, back_ref, staged, sems):
    place = lax.axis_index("ep")
    crossing, which = place % 2 == 1, (place // SPAN).astype(F32)
    half_width = rows_ref.shape[1] - EXTRA
    total = ALONG * TIGHT
    tail = rows_ref[:, half_width:].astype(F32)
    named = jnp.where((tail > 0.0) & (index((WIDE, EXTRA), 1) < EXPERTS - 0.5), 1.0, 0.0)
    one, two = index((WIDE, WIDE), 0), index((WIDE, WIDE), 1)
    ahead = jnp.where((split(one, ROWS)[0] == split(two, ROWS)[0]) & (two < one), 1.0, 0.0)
    rank = jnp.dot(ahead.astype(BF16), named.astype(BF16), preferred_element_type=F32)
    code = jnp.where(named > 0.5, rank, -1.0).astype(BF16)

    def matrix(found, at, to):
        source, slot = split(split(at, TIGHT)[1], MOST)
        block = split(to, ROWS)[0]
        return jnp.where((block == source) & (found == slot), 1.0, 0.0).astype(BF16)

    def pick(at, to):
        target = jnp.where(crossing, split(at, TIGHT)[0], which)
        return jnp.where(to == target, 1.0, 0.0).astype(BF16)

    chosen = pick(index((total, 1), 0), index((total, EXTRA), 1))
    found = lax.dot_general(chosen, code, (((1,), (1,)), ((), ())), preferred_element_type=F32)
    forth = matrix(found, index((total, 1), 0), index((1, WIDE), 1))
    copies = []
    for k, lo in enumerate(range(0, half_width, CHUNK)):
        at = pl.ds(lo, min(CHUNK, half_width - lo))
        staged[:, at] = jnp.dot(forth, rows_ref[:, at], preferred_element_type=F32).astype(BF16)
        copies.append(pltpu.make_async_copy(staged.at[:, at], out_ref.at[:, at], sems.at[k]))
        copies[k].start()
    chosen = pick(index((1, total), 1), index((EXTRA, total), 0))
    found = jnp.dot(code, chosen, preferred_element_type=F32)
    here = matrix(found, index((1, total), 1), index((WIDE, 1), 0)).astype(F32)
    exact = rows_ref[:, half_width:]
    high = jnp.dot(exact, chosen, preferred_element_type=F32)
    chosen = pick(index((1, total), 1), index((EXTRA, total), 0) - EXPERTS)
    low = jnp.dot(exact, chosen, preferred_element_type=F32)
    back_ref[:WIDE] = (here * high).astype(BF16)
    back_ref[WIDE:] = (here * low).astype(BF16)
    for copy in copies:
        copy.wait()


def gate(
    rows_ref, gain_ref, own_ref, other_hbm, kept_ref, sent_ref, squares_ref, other_ref, sems
):
    half_width, cols = own_ref.shape[0], kept_ref.shape[1]
    rows = rows_ref.shape[0]
    deep = half_width // PIECES
    copies = []
    for k in range(PIECES):
        at = pl.ds(k * deep, deep)
        copies.append(pltpu.make_async_copy(other_hbm.at[at], other_ref.at[at], sems.at[k]))
        copies[k].start()
    for k in range(PIECES):
        at = slice(k * deep, (k + 1) * deep)
        values = rows_ref[:, at].astype(F32)
        pieces = values * values
        part = pieces[:, :EXTRA]
        for lo in range(EXTRA, deep, EXTRA):
            part = part + pieces[:, lo : lo + EXTRA]
        squares_ref[...] = part + (squares_ref[...] if k else 0.0)
        scaled = (values * gain_ref[:, at].astype(F32)).astype(BF16)
        sums = jnp.dot(scaled, own_ref[at, :], preferred_element_type=F32)
        kept_ref[:, : cols // 2] = sums + (kept_ref[:, : cols // 2] if k else 0.0)
        copies[k].wait()
        sums = jnp.dot(scaled, other_ref[at, :], preferred_element_type=F32)
        kept_ref[:, cols // 2 :] = sums + (kept_ref[:, cols // 2 :] if k else 0.0)
    squares = jnp.sum(squares_ref[...], axis=1, keepdims=True)
    squares_ref[...] = jnp.broadcast_to(squares, squares_ref.shape)
    sent_ref[:rows] = kept_ref[...].astype(BF16)
    across = lax.broadcasted_iota(jnp.int32, (rows, cols), 1)
    down = lax.broadcasted_iota(jnp.int32, (rows, cols), 0)
    total = jnp.sum(jnp.where(across == down, squares, 0.0), axis=0, keepdims=True)
    high = total.astype(BF16).astype(F32)
    row = lax.broadcasted_iota(jnp.int32, (16, cols), 0)
    sent_ref[rows:] = jnp.where(row == 0, high, jnp.where(row == 1, total - high, 0.0)).astype(BF16)


def expert(width, kept_ref, squares_ref, got_ref, down_ref, out_ref):
    units, half_width = down_ref.shape[0] // 2, down_ref.shape[1]
    rows = kept_ref.shape[0]
    far = jnp.sum(got_ref[rows:].astype(F32), axis=0, keepdims=True)
    across = lax.broadcasted_iota(jnp.int32, (rows, far.shape[1]), 1)
    same = across == lax.broadcasted_iota(jnp.int32, (rows, far.shape[1]), 0)
    squares = squares_ref[:, :1] + jnp.sum(jnp.where(same, far, 0.0), axis=1, keepdims=True)
    scale = lax.rsqrt(squares * (1.0 / width) + 1e-06)
    hidden = []
    for at in range(2):
        lo = 2 * units * at
        a = (kept_ref[:, lo : lo + units] + got_ref[:rows, lo : lo + units].astype(F32)) * scale
        lo += units
        b = (kept_ref[:, lo : lo + units] + got_ref[:rows, lo : lo + units].astype(F32)) * scale
        hidden.append((a / (1.0 + jnp.exp(-a)) * b).astype(BF16))
    both = jnp.concatenate(hidden, axis=1)
    deep = half_width // 2
    for k in range(2):
        at = slice(k * deep, (k + 1) * deep)
        out_ref[:, at] = jnp.dot(both, down_ref[:, at], preferred_element_type=F32).astype(BF16)


def gather_parts(back_ref, parts_ref, out_ref):
    sums = jnp.dot(back_ref[...], parts_ref[...], preferred_element_type=F32)
    sums = (sums[:WIDE] + sums[WIDE:]).astype(BF16)
    for t in range(ALONG):
        out_ref[t] = sums[t * ROWS : (t + 1) * ROWS]


def finish(parts_ref, rows_ref, out_ref, sent_ref):
    half_width = rows_ref.shape[1]
    mixture = parts_ref[0].astype(F32)
    for t in range(1, ALONG):
        mixture += parts_ref[t].astype(F32)
    layer = (rows_ref[...].astype(F32) + mixture).astype(BF16)
    out_ref[...] = layer
    values = layer.astype(F32)
    total = jnp.sum(values * values, axis=1, keepdims=True)
    high = total.astype(BF16).astype(F32)
    lane = lax.broadcasted_iota(jnp.int32, (ROWS, EXTRA), 1)
    pieces = jnp.where(lane == 0, high, jnp.where(lane == 1, total - high, 0.0)).astype(BF16)
    for to in range(sent_ref.shape[0]):
        sent_ref[to, :, :half_width] = layer
        sent_ref[to, :, half_width:] = pieces


def close(width, got_ref, gain_ref, out_ref):
    half_width = gain_ref.shape[1]
    crossed, side = 1 - lax.axis_index("section"), lax.axis_index("tp")
    values = got_ref[crossed * 2 + side, :, :half_width].astype(F32)
    far = got_ref[crossed * 2 + 1 - side, :, half_width:].astype(F32)
    total = jnp.sum(values * values, axis=1, keepdims=True) + jnp.sum(far, axis=1, keepdims=True)
    scale = lax.rsqrt(total * (1.0 / width) + 1e-06)
    out_ref[...] = (values * scale * gain_ref[...].astype(F32)).astype(BF16)


def local(kernel, outs, *args, spaces=None, out_spaces=None, scratch=(), vmem=24 * MIB):
    spaces = spaces or [pltpu.VMEM] * len(args)
    out_spaces = out_spaces or [pltpu.VMEM] * len(outs)
    return pl.pallas_call(
        kernel,
        out_shape=outs,
        in_specs=[pl.BlockSpec(memory_space=space) for space in spaces],
        out_specs=[pl.BlockSpec(memory_space=space) for space in out_spaces],
        scratch_shapes=list(scratch),
        compiler_params=pltpu.CompilerParams(vmem_limit_bytes=vmem),
    )(*args)


def shape(*dims, dtype=BF16):
    return jax.ShapeDtypeStruct(dims, dtype)


def body(section_rows, routes, route_weights, in_gain, gate_up, down, out_gain):
    rows = section_rows[0]
    half_width = rows.shape[1]
    ep = lax.axis_size("ep")
    width = half_width * lax.axis_size("tp")
    units = down.shape[2]
    cols = gate_up.shape[3]
    near, far = crossed_groups(ep, 1), crossed_groups(ep, 0)
    other_core = [(i, i ^ 1) for i in range(ep)]
    swap = [(0, 1), (1, 0)]
    full = half_width + EXTRA
    total = ALONG * TIGHT

    gate_own, down_own = gate_up[0, 0], down[0, 0]
    gate_other = lax.ppermute(gate_own, "ep", other_core)
    down_other = lax.ppermute(down_own, "ep", other_core)
    gain_other = lax.ppermute(out_gain, "section", swap)

    down_all = jnp.concatenate([down_own, down_other], axis=0)

    (leaving,) = local(
        announce,
        [shape(ALONG, ROWS, full)],
        rows,
        routes[0],
        route_weights[0],
        vmem=60 * MIB,
    )
    met = traded(leaving, near).reshape(WIDE, full)
    sorted_rows, far_back = local(
        sort_rows,
        [shape(total, half_width), shape(2 * WIDE, total)],
        met,
        out_spaces=[pltpu.HBM, pltpu.VMEM],
        scratch=[
            pltpu.VMEM((total, half_width), BF16),
            pltpu.SemaphoreType.DMA((-(-half_width // CHUNK),)),
        ],
        vmem=53 * MIB,
    )
    gathered = traded(sorted_rows.reshape(ALONG, TIGHT, half_width), far)
    gathered = gathered.reshape(total, half_width)
    gathered, gain_other = lax.optimization_barrier((gathered, gain_other))
    kept, sent, squares = local(
        gate,
        [
            shape(total, 2 * cols, dtype=F32),
            shape(total + 16, 2 * cols),
            shape(total, EXTRA, dtype=F32),
        ],
        gathered,
        in_gain,
        gate_own,
        gate_other,
        spaces=[pltpu.VMEM] * 3 + [pl.ANY],
        scratch=[
            pltpu.VMEM((half_width, cols), BF16),
            pltpu.SemaphoreType.DMA((PIECES,)),
        ],
    )
    got = lax.ppermute(sent, "tp", swap)
    (parts,) = local(
        functools.partial(expert, width),
        [shape(total, half_width)],
        kept,
        squares,
        got,
        down_all,
    )
    returned = traded(parts.reshape(ALONG, TIGHT, half_width), far).reshape(total, half_width)
    (summed,) = local(gather_parts, [shape(ALONG, ROWS, half_width)], far_back, returned)
    home = traded(summed, near)
    layer_out, leaving = local(
        finish, [shape(ROWS, half_width), shape(4, ROWS, full)], home, rows
    )
    got = lax.all_to_all(leaving, ("section", "tp"), 0, 0, tiled=True)
    (handed,) = local(
        functools.partial(close, width),
        [shape(ROWS, half_width)],
        got,
        gain_other,
    )
    return (layer_out[None], handed[None])


def solution(mesh):
    return jax.shard_map(
        body,
        mesh=mesh,
        in_specs=(
            P("section", "ep", "tp"),
            P("section", "ep", None),
            P("section", "ep", None),
            P("section", "tp"),
            P("section", "ep", "tp", None),
            P("section", "ep", None, "tp"),
            P("section", "tp"),
        ),
        out_specs=(P("section", "ep", "tp"), P("section", "ep", "tp")),
        check_vma=False,
    )
```
